256 devices in a mesh: rows: 4 (over y_lo, core), gr: 8 (over x, y_hi), gc: 8 (over z).
Axes of the slice: x: 4, y: 4 (y_hi: 2, y_lo: 2; y = y_hi * 2 + y_lo), z: 8, core: 2. Of those that a mesh axis runs over, the one named last changes fastest.
Arguments:
- samples: float32 [2048, 8192], P(('rows', 'gc'), 'gr'), may hold values from -6 to 6
- targets: float32 [2048], P(('rows', 'gc')), may hold values from -6 to 6
- ridge: float32 [8192], P('gr'), may hold values from 0.5 to 2
Outputs:
- trailing: float32 [8192, 8192], P('gr', 'gc')
- panel: float32 [8192, 512], P('gr')
- reduced_rhs: float32 [8192], P('gr')
The draws below stay inside these ranges and needn't reach their ends.
All inputs are finite; a program needn't handle non-finite values.
Results may differ from the reference program's by a relative error of at most 0.00011.
Values sent between devices are 32-bit elements; how exact they have to be, the bound alone decides.
A program may use at most 64 MiB of HBM per device.

```python
import math
import jax
import jax.numpy as jnp
from jax import lax

F = 8192
PANEL = 512
SAMPLES = 2048


def level_of(key, extent, pieces, least, high):
    def one(dim, blocks):
        heights = jax.random.uniform(jax.random.fold_in(jax.random.fold_in(key, 6), dim), (blocks,), jnp.float32, least / len(pieces), high / len(pieces))
        return jnp.repeat(jnp.exp(heights), extent[dim] // blocks).reshape((-1,) + (1,) * (len(extent) - dim - 1))

    loudness = one(*pieces[0])
    for cut in pieces[1:]:
        loudness = loudness * one(*cut)
    return loudness


def gaussian(key, extent, spread, reach, shards=(), dtype=jnp.bfloat16):
    result = spread * jax.random.normal(key, extent, jnp.float32)
    if shards:
        result = result * level_of(key, extent, shards, -0.22, 0.18)
    return jnp.clip(result, -reach, reach).astype(dtype)


def setup_inputs(seed: int = 0) -> dict:
    seeds = jax.random.split(jax.random.key(seed), 4)
    samples = gaussian(seeds[0], (SAMPLES, F), 1.0, 6.0, ((0, 32), (1, 8)), jnp.float32)
    targets = gaussian(seeds[1], (SAMPLES,), 1.0, 6.0, ((0, 32),), jnp.float32)
    ridge = jnp.clip(jnp.exp(math.log(2.0) - 1.3862944 * jax.random.uniform(seeds[2], (F,), jnp.float32) ** level_of(seeds[2], (F,), ((0, 8),), -0.2, 0.2)), 0.5, 2.0)
    return {"samples": samples, "targets": targets, "ridge": ridge}


def reference(samples, targets, ridge):
    count = samples.shape[0]
    highest = lax.Precision.HIGHEST
    gram = jnp.dot(samples.T.astype(jnp.float32), samples.astype(jnp.float32), precision=highest, preferred_element_type=jnp.float32) / count
    diagonal_index = jnp.arange(F)
    gram = gram.at[diagonal_index, diagonal_index].add(ridge)
    rhs = jnp.dot(targets.astype(jnp.float32), samples.astype(jnp.float32), precision=highest, preferred_element_type=jnp.float32) / count
    top = jnp.linalg.cholesky(gram[:PANEL, :PANEL])
    panel = jax.scipy.linalg.solve_triangular(top, gram[:, :PANEL].T, lower=True).T
    trailing = gram - jnp.dot(panel.astype(jnp.float32), panel.T.astype(jnp.float32), precision=highest, preferred_element_type=jnp.float32)
    solved = jax.scipy.linalg.solve_triangular(top, rhs[:PANEL], lower=True)
    reduced_rhs = rhs - jnp.dot(panel.astype(jnp.float32), solved.astype(jnp.float32), precision=highest, preferred_element_type=jnp.float32)
    return (trailing, panel, reduced_rhs)
```

```python
import jax
import jax.numpy as jnp
from jax import lax
from jax.experimental import pallas as pl
from jax.experimental.pallas import tpu as pltpu
from jax.sharding import PartitionSpec as P

f32, bf16 = jnp.float32, jnp.bfloat16
MESH = pl.DeviceIdType.MESH
PANEL = 512
W = 1024
K = 2048
NZ = 8
N = 128


def fdot(a, b, dims=((1,), (0,))):
    return lax.dot_general(a, b, (dims, ((), ())), precision=lax.Precision.HIGHEST, preferred_element_type=f32)


def bdot(a, b, dims=((1,), (0,))):
    return lax.dot_general(a, b, (dims, ((), ())), preferred_element_type=f32)


def high_low(x):
    high = x.astype(bf16)
    return high, (x - high.astype(f32)).astype(bf16)


def split3(x):
    a = x.astype(bf16).astype(f32)
    r = x - a
    b = r.astype(bf16).astype(f32)
    return a, b, r - b


def stack_left(x):
    a, b, c = split3(x)
    return jnp.concatenate([a, a, a, b, b, c], 0).astype(bf16)


def stack_right(x):
    a, b, c = split3(x)
    return jnp.concatenate([a, b, c, a, b, a], 0).astype(bf16)


def dot3(a, b, dims):
    (da,), (db,) = dims
    ah, al = high_low(a)
    bh, bl = high_low(b)
    return bdot(jnp.concatenate([ah, al, ah], da), jnp.concatenate([bh, bh, bl], db), dims)


def row_of(x, i):
    return jnp.broadcast_to(x[i : i + 1, :], (8, x.shape[1]))


def twice(x):
    return jnp.concatenate([x, x], 1)


def strip_factor(s, strip):
    left = strip[:, :N]
    cols = [jnp.take_along_axis(left, jnp.full((8, N), s * 8 + j, jnp.int32), axis=1) for j in range(8)]
    e = {(i, j): row_of(cols[j], i) for j in range(8) for i in range(j, 8)}
    t = [row_of(strip, i) for i in range(8)]
    f, inv, root = {}, [], []
    for k in range(8):
        r = lax.rsqrt(e[k, k])
        r = r * (1.5 - 0.5 * e[k, k] * r * r)
        p = r * r
        p = p * (2.0 - e[k, k] * p)
        inv.append(p)
        root.append(r)
        for i in range(k + 1, 8):
            f[i, k] = e[i, k] * p
        for j in range(k + 1, 8):
            for i in range(j, 8):
                e[i, j] = e[i, j] - f[i, k] * e[j, k]
        for i in range(k + 1, 8):
            t[i] = t[i] - twice(f[i, k]) * t[k]
    y = [None] * 8
    for i in reversed(range(8)):
        acc = t[i] * twice(inv[i])
        for k in range(i + 1, 8):
            acc = acc - twice(f[k, i]) * y[k]
        y[i] = acc
    row = lax.broadcasted_iota(jnp.int32, (8, N), 0)

    def assemble(parts):
        out = parts[0]
        rows = row if out.shape[1] == N else twice(row)
        for i in range(1, 8):
            out = jnp.where(rows == i, parts[i], out)
        return out

    return assemble(y), assemble([t[i][:, N:] * root[i] for i in range(8)]), y


def factor_block(ab, m_ref):
    def body(s, carry):
        strip, left, right = carry
        ab[...] = ab[...] - bdot(left, right)
        whole, inverse_rows, y = strip_factor(s, strip)
        m_ref[pl.ds(pl.multiple_of(s * 8, 8), 8), :] = inverse_rows
        after = lax.rem(s + 1, 16)
        rows = ab[pl.ds(pl.multiple_of(after * 8, 8), 8), :]
        terms = []
        for j in range(8):
            c = jnp.take_along_axis(rows[:, :N], jnp.full((8, N), s * 8 + j, jnp.int32), axis=1)
            terms.append(twice(c) * y[j])
        while len(terms) > 1:
            terms = [terms[i] + terms[i + 1] for i in range(0, len(terms), 2)]
        return rows - terms[0], stack_left(strip[:, :N]).T, stack_right(whole)

    lax.fori_loop(0, 16, body, (ab[0:8, :], jnp.zeros((N, 48), bf16), jnp.zeros((48, 2 * N), bf16)))


def factor_inverse(a, b, ab, m):
    b[...] = jnp.zeros_like(b)
    eye = jnp.where(
        lax.broadcasted_iota(jnp.int32, (N, N), 0) == lax.broadcasted_iota(jnp.int32, (N, N), 1), 1.0, 0.0
    )
    blocks = PANEL // N
    for k in range(blocks):
        now, rest = slice(k * N, (k + 1) * N), slice((k + 1) * N, PANEL)
        ab[:, :N] = a[now, now]
        ab[:, N:] = eye
        factor_block(ab, m)
        b[now, now] = m[...]
        if k:
            b[now, : k * N] = fdot(m[...], b[now, : k * N])
        if k < blocks - 1:
            u = fdot(m[...], a[now, rest])
            a[rest, rest] = a[rest, rest] - fdot(u, u, ((0,), (0,)))
            b[rest, : (k + 1) * N] = b[rest, : (k + 1) * N] - fdot(u, b[now, : (k + 1) * N], ((0,), (0,)))


def gather_kernel(
    samp, targ, ridge,
    tpre_o, gi0_o, g0j_o, g00_o, rhs_o, top_o, ridge_o,
    chunk, ai, sj, zb, rg, ah, al, jh, jl, zh, zl, tpre, gi0, g0j, g00, rhs, top,
    ex_s, ex_r, ye_s, ye_r, si_s, si_r, sc_s, sc_r, zs_s, zs_r, rg_s, rg_r, zz_s, zz_r, ag_s, ag_r, d_s, d_r, o_s, o_r, lo,
):
    r, i, z = lax.axis_index("rows"), lax.axis_index("gr"), lax.axis_index("gc")
    core, yl = lax.rem(r, 2), r // 2
    x, yh = i // 2, lax.rem(i, 2)
    y = yh * 2 + yl
    p = y * 4 + x
    q = z * 2 + yl
    first, second = core == 0, core == 1

    def dev(xx, yy, zz, c):
        return {"rows": lax.rem(yy, 2) * 2 + c, "gr": xx * 2 + yy // 2, "gc": zz}

    def up(v, n):
        return lax.rem(v + 1, n)

    def down(v, n):
        return lax.rem(v + n - 1, n)

    sibling = dev(x, y, z, 1 - core)

    barrier = pltpu.get_barrier_semaphore()

    def greet(device):
        pl.semaphore_signal(barrier, inc=1, device_id=device, device_id_type=MESH)

    greet(sibling)
    for xx, yy in ((up(x, 4), y), (down(x, 4), y), (x, up(y, 4)), (x, down(y, 4))):
        greet(dev(xx, yy, z, core))

    own_plane = jnp.where(i == z, 1, 0)
    source = jnp.where(i == 0, 1, 0)

    @pl.when(second)
    def _():
        greet(dev(x, y, up(z, NZ), 1))
        greet(dev(x, y, down(z, NZ), 1))
        for b in range(2):
            for zz in range(NZ):
                is_self = jnp.logical_and(i == z, jnp.logical_and(yl == b, z == zz))

                @pl.when(jnp.logical_not(is_self))
                def _():
                    greet({"rows": b * 2 + 1, "gr": z, "gc": zz})

        pl.semaphore_wait(barrier, 23 - own_plane)

    @pl.when(first)
    def _():
        for d in range(1, NZ):
            greet(dev(x, y, lax.rem(z + d, NZ), 0))
        for b in range(2):

            @pl.when(jnp.logical_not(jnp.logical_and(i == 0, yl == b)))
            def _():
                greet({"rows": b * 2, "gr": 0, "gc": z})

        pl.semaphore_wait(barrier, 12 + 15 * source)

    mine = pl.ds(pl.multiple_of(core * 64, 64), 64)
    theirs = pl.ds(pl.multiple_of((1 - core) * 64, 64), 64)
    chunk[mine, :W] = samp[...]
    chunk[mine, W:] = targ[...]
    swap = pltpu.make_async_remote_copy(
        chunk.at[mine], chunk.at[mine], ex_s, ex_r, device_id=sibling, device_id_type=MESH
    )
    swap.start()
    pltpu.make_async_remote_copy(
        chunk.at[theirs], chunk.at[theirs], ex_s, ex_r, device_id=sibling, device_id_type=MESH
    ).wait_recv()
    own = ai.at[z, yl]
    for b in range(W // N):
        own[b * N : (b + 1) * N, :] = chunk[:, b * N : (b + 1) * N].T
    own[W : W + 8, :] = chunk[:, W:].T[:8]
    lanes = pl.ds(pl.multiple_of(q * N, N), N)

    def plane(buf, c, half_rows):
        sub = half_rows // 2

        def move(h, index, u_off, v_off, off, size, du, dv):
            a, b = (x, y) if h == 0 else (y, x)
            uu, vv = lax.rem(a + u_off + 4, 4), lax.rem(b + v_off + 4, 4)
            tu, tv = lax.rem(a + du + 4, 4), lax.rem(b + dv + 4, 4)
            rows = pl.ds(h * half_rows + off, size)
            item = buf.at[vv, uu, rows] if h == 0 else buf.at[uu, vv, rows]
            to = dev(tu, tv, z, c) if h == 0 else dev(tv, tu, z, c)
            return pltpu.make_async_remote_copy(
                item, item, ag_s.at[h, index], ag_r.at[h, index], device_id=to, device_id_type=MESH
            )

        offsets = (0, -1, 1, 2)

        def u_send(h, n):
            return (
                lambda: move(h, 0, 0, 0, 0, half_rows, 1, 0),
                lambda: move(h, 1, 0, 0, 0, half_rows, -1, 0),
                lambda: move(h, 2, -1, 0, 0, sub, 1, 0),
                lambda: move(h, 3, 1, 0, sub, sub, -1, 0),
            )[n]()

        def u_recv(h, n):
            return (
                lambda: move(h, 0, -1, 0, 0, half_rows, 1, 0),
                lambda: move(h, 1, 1, 0, 0, half_rows, -1, 0),
                lambda: move(h, 2, -2, 0, 0, sub, 1, 0),
                lambda: move(h, 3, 2, 0, sub, sub, -1, 0),
            )[n]()

        def v_send(h, o, n):
            at, u = 4 + 4 * o, offsets[o]
            return (
                lambda: move(h, at, u, 0, 0, half_rows, 0, 1),
                lambda: move(h, at + 1, u, 0, 0, half_rows, 0, -1),
                lambda: move(h, at + 2, u, -1, 0, sub, 0, 1),
                lambda: move(h, at + 3, u, 1, sub, sub, 0, -1),
            )[n]()

        def v_recv(h, o, n):
            at, u = 4 + 4 * o, offsets[o]
            return (
                lambda: move(h, at, u, -1, 0, half_rows, 0, 1),
                lambda: move(h, at + 1, u, 1, 0, half_rows, 0, -1),
                lambda: move(h, at + 2, u, -2, 0, sub, 0, 1),
                lambda: move(h, at + 3, u, 2, sub, sub, 0, -1),
            )[n]()

        def both(step):
            def run():
                for h in range(2):
                    step(h)

            return run

        def begin(h):
            u_send(h, 0).start()
            u_send(h, 1).start()
            v_send(h, 0, 0).start()
            v_send(h, 0, 1).start()

        def u_first(h):
            for n in range(2):
                u_recv(h, n).wait_recv()
                u_send(h, n + 2).start()
                v_send(h, n + 1, 0).start()
                v_send(h, n + 1, 1).start()

        def v_forward(o):
            def step(h):
                for n in range(2):
                    v_recv(h, o, n).wait_recv()
                    v_send(h, o, n + 2).start()

            return step

        def u_second(h):
            u_recv(h, 2).wait_recv()
            u_recv(h, 3).wait_recv()
            v_send(h, 3, 0).start()
            v_send(h, 3, 1).start()

        def end(h):
            for o in range(4):
                v_recv(h, o, 2).wait_recv()
                v_recv(h, o, 3).wait_recv()

        def sent(h):
            for n in range(4):
                u_send(h, n).wait_send()
                for o in range(4):
                    v_send(h, o, n).wait_send()

        return [both(s) for s in (begin, u_first, v_forward(0), u_second, v_forward(1), v_forward(2), v_forward(3), end, sent)]

    def away(n, src, dst):
        return pltpu.make_async_remote_copy(
            src, dst, o_s.at[n], o_r.at[n], device_id=sibling, device_id_type=MESH
        )

    def here(n, src, dst):
        return pltpu.make_async_copy(src, dst, lo.at[n])

    from_second = ((tpre, tpre_o), (gi0, gi0_o), (g0j, g0j_o), (rhs, rhs_o), (top, top_o))
    from_first = ((g00, g00_o), (rg, ridge_o))

    z_over = pltpu.make_async_remote_copy(zb, zb, d_s, d_r, device_id=sibling, device_id_type=MESH)

    @pl.when(first)
    def _():
        def z_piece(b, pp):
            yy, xx = pp // 4, pp % 4
            return pltpu.make_async_remote_copy(
                own.at[pl.ds(pp * 32, 32)],
                zb.at[yy, xx, :, lanes],
                zs_s.at[pp],
                zs_r.at[yl],
                device_id=dev(xx, yy, z, 0),
                device_id_type=MESH,
            )

        def r_piece(pp):
            yy, xx = pp // 4, pp % 4
            return pltpu.make_async_remote_copy(
                rg, rg, rg_s.at[pp], rg_r, device_id=dev(xx, yy, z, 0), device_id_type=MESH
            )

        @pl.when(i == 0)
        def _():
            @pl.when(yl == 0)
            def _():
                rg[...] = ridge[:, :PANEL]

            for pp in range(16):

                @pl.when(p == pp)
                def _():
                    pltpu.make_async_copy(
                        own.at[pl.ds(pp * 32, 32)], zb.at[pp // 4, pp % 4, :, lanes], zs_r.at[yl]
                    ).start()

                @pl.when(p != pp)
                def _():
                    z_piece(0, pp).start()

                    @pl.when(yl == 0)
                    def _():
                        r_piece(pp).start()

        for b in range(2):
            at = zb.at[y, x, :, pl.ds(pl.multiple_of((z * 2 + b) * N, N), N)]
            pltpu.make_async_copy(at, at, zs_r.at[b]).wait()
        pair = zb.at[y, x, :, pl.ds(pl.multiple_of(z * 2 * N, 2 * N), 2 * N)]

        def along(d):
            return pltpu.make_async_remote_copy(
                pair, pair, zz_s.at[d - 1], zz_r.at[d - 1],
                device_id=dev(x, y, lax.rem(z + d, NZ), 0), device_id_type=MESH,
            )

        for d in (1, 7, 2, 6, 3, 5, 4):
            along(d).start()
        for d in (1, 7, 2, 6, 3, 5, 4):
            at = zb.at[y, x, :, pl.ds(pl.multiple_of(lax.rem(z - d + NZ, NZ) * 2 * N, 2 * N), 2 * N)]
            pltpu.make_async_remote_copy(
                at, at, zz_s.at[d - 1], zz_r.at[d - 1], device_id=sibling, device_id_type=MESH
            ).wait_recv()
        steps = plane(zb, 0, 16)
        for step in steps[:-1]:
            step()
        z_over.start()

        for b in range(2):
            rows = slice(b * 8, (b + 1) * 8)
            part = fdot(
                zb[b * 2 : b * 2 + 2].reshape(256, K), zb[...].reshape(PANEL, K), ((1,), (1,))
            )
            g00[b * 256 : (b + 1) * 256, :] = part * (1.0 / K)

        @pl.when(jnp.logical_not(jnp.logical_and(i == 0, yl == 0)))
        def _():
            r_piece(0).wait_recv()

        row = lax.broadcasted_iota(jnp.int32, (PANEL, PANEL), 0)
        col = lax.broadcasted_iota(jnp.int32, (PANEL, PANEL), 1)
        g00[...] = g00[...] + jnp.where(row == col, rg[0:1, :], 0.0)
        for n, (src, dst) in enumerate(from_first):
            away(5 + n, src, dst).start()
            here(5 + n, src, dst).start()

        steps[-1]()
        for d in range(1, NZ):
            along(d).wait_send()

        @pl.when(i == 0)
        def _():
            for pp in range(16):

                @pl.when(p != pp)
                def _():
                    z_piece(0, pp).wait_send()

                    @pl.when(yl == 0)
                    def _():
                        r_piece(pp).wait_send()

        z_over.wait_send()
        for n, (src, dst) in enumerate(from_first):
            away(5 + n, src, dst).wait_send()
            here(5 + n, src, dst).wait()
        for n, (src, dst) in enumerate(from_second):
            away(n, src, dst).wait_recv()

    @pl.when(second)
    def _():
        def ring(way, s, part):
            at = lax.rem(z - s + 1 + NZ, NZ) if way == 0 else lax.rem(z + s - 1, NZ)
            to = dev(x, y, up(z, NZ) if way == 0 else down(z, NZ), 1)
            which = yl if part == 0 else 1 - yl
            item = ai.at[at, which]
            return pltpu.make_async_remote_copy(
                item, item, si_s.at[way, s - 1, part], si_r.at[way, s - 1, part], device_id=to, device_id_type=MESH
            )

        def ring_in(way, s, part):
            at = lax.rem(z - s + NZ, NZ) if way == 0 else lax.rem(z + s, NZ)
            which = yl if part == 0 else 1 - yl
            item = ai.at[at, which]
            return pltpu.make_async_remote_copy(
                item, item, si_s.at[way, s - 1, part], si_r.at[way, s - 1, part], device_id=sibling, device_id_type=MESH
            )

        ring_list = [(s, part, way) for s in (1, 2, 3) for part in range(2) for way in range(2)] + [(4, 0, 0), (4, 1, 1)]

        def s_piece(pp):
            yy, xx = pp // 4, pp % 4
            return pltpu.make_async_remote_copy(
                own.at[pl.ds(pp * 64, 64)],
                sj.at[yy, xx, :, lanes],
                sc_s.at[pp],
                sc_r.at[q],
                device_id=dev(xx, yy, i, 1),
                device_id_type=MESH,
            )

        for pp in range(16):
            is_self = jnp.logical_and(i == z, p == pp)

            @pl.when(is_self)
            def _():
                pltpu.make_async_copy(
                    own.at[pl.ds(pp * 64, 64)], sj.at[pp // 4, pp % 4, :, lanes], sc_r.at[q]
                ).start()

            @pl.when(jnp.logical_not(is_self))
            def _():
                s_piece(pp).start()

        partner = dev(x, yh * 2 + 1 - yl, z, 1)
        trade = pltpu.make_async_remote_copy(own, own, ye_s, ye_r, device_id=partner, device_id_type=MESH)
        trade.start()
        ring(0, 1, 0).start()
        ring(1, 1, 0).start()

        for n in range(16):
            at = sj.at[y, x, :, pl.ds(n * N, N)]
            pltpu.make_async_copy(at, at, sc_r.at[n]).wait()
        steps = plane(sj, 1, 32)

        def advance(s, part, way):
            ring_in(way, s, part).wait_recv()
            if (s + 1, part, way) in ring_list:
                ring(way, s + 1, part).start()

        steps[0]()
        other = ai.at[z, 1 - yl]
        pltpu.make_async_remote_copy(other, other, ye_s, ye_r, device_id=partner, device_id_type=MESH).wait_recv()
        ring(0, 1, 1).start()
        ring(1, 1, 1).start()
        moves = list(ring_list)
        for step in steps[1:-1]:
            for _ in range(2):
                advance(*moves.pop(0))
            step()
        z_over.wait_recv()

        def split_j(n, c):
            for rows in range(2):
                part = pl.ds(pl.multiple_of(n * 64 + rows * 32, 32), 32)
                h, l = high_low(sj[n // 4, lax.rem(n, 4), rows * 32 : rows * 32 + 32, :])
                jh[part, :] = h
                jl[part, :] = l
            part = pl.ds(pl.multiple_of(n * 32, 32), 32)
            h, l = high_low(zb[n // 4, lax.rem(n, 4)])
            zh[part, :] = h
            zl[part, :] = l
            return c

        lax.fori_loop(0, 16, split_j, 0)
        while moves:
            advance(*moves.pop(0))

        def split_i(n, c):
            rows = pl.ds(pl.multiple_of(n * N, N), N)
            for zz in range(NZ):
                for b in range(2):
                    h, l = high_low(ai[zz, b, rows, :])
                    ah[zz, rows, b * N : (b + 1) * N] = h
                    al[zz, rows, b * N : (b + 1) * N] = l
            return c

        lax.fori_loop(0, W // N, split_i, 0)

        tpre[...] = jnp.zeros_like(tpre)
        gi0[...] = jnp.zeros_like(gi0)
        g0j[...] = jnp.zeros_like(g0j)
        rhs[...] = jnp.zeros_like(rhs)
        top[...] = jnp.zeros_like(top)

        def products(zz, c):
            ks = pl.ds(pl.multiple_of(zz * 256, 256), 256)
            across = ((1,), (1,))
            t = jnp.concatenate([ai[zz, 0, W : W + 8, :], ai[zz, 1, W : W + 8, :]], 1)
            th, tl = high_low(t)
            tc = jnp.concatenate([th, tl, th], 1)

            def a_cat(rows, order):
                h, l = ah[zz, rows, :], al[zz, rows, :]
                return jnp.concatenate([h, l, h] if order == 0 else [h, h, l], 1)

            def z_cat(rows, order):
                h, l = zh[rows, ks], zl[rows, ks]
                return jnp.concatenate([h, l, h] if order == 0 else [h, h, l], 1)

            every = pl.ds(0, W)
            half = pl.ds(0, PANEL)

            def columns(n, c):
                rows = pl.ds(pl.multiple_of(n * 256, 256), 256)
                right = jnp.concatenate([jh[rows, ks], jh[rows, ks], jl[rows, ks]], 1)
                tpre[:, rows] += bdot(a_cat(every, 0), right, across)
                g0j[:, rows] += bdot(z_cat(half, 0), right, across)
                rhs[:, rows] += bdot(tc, a_cat(rows, 1), across)
                return c

            lax.fori_loop(0, 4, columns, 0)

            def panel_columns(n, c):
                rows = pl.ds(pl.multiple_of(n * 256, 256), 256)
                right = z_cat(rows, 1)
                gi0[:, rows] += bdot(a_cat(every, 0), right, across)
                top[:, rows] += bdot(tc, right, across)
                return c

            lax.fori_loop(0, 2, panel_columns, 0)
            return c

        lax.fori_loop(0, NZ, products, 0)

        for n, (src, dst) in enumerate(from_second):
            away(n, src, dst).start()
            here(n, src, dst).start()
        steps[-1]()
        for s, part, way in ring_list:
            ring(way, s, part).wait_send()
        trade.wait_send()
        for pp in range(16):
            is_self = jnp.logical_and(i == z, p == pp)

            @pl.when(jnp.logical_not(is_self))
            def _():
                s_piece(pp).wait_send()

        for n, (src, dst) in enumerate(from_second):
            away(n, src, dst).wait_send()
            here(n, src, dst).wait()
        for n, (src, dst) in enumerate(from_first):
            away(5 + n, src, dst).wait_recv()

    swap.wait_send()


def gather(samples, targets, ridge):
    anywhere = pl.BlockSpec(memory_space=pl.ANY)
    inside = pl.BlockSpec(memory_space=pltpu.VMEM)
    dma = pltpu.SemaphoreType.DMA
    shapes = [(W, W), (W, PANEL), (PANEL, W), (PANEL, PANEL), (8, W), (8, PANEL), (8, PANEL)]
    return pl.pallas_call(
        gather_kernel,
        out_shape=[jax.ShapeDtypeStruct(s, f32) for s in shapes],
        in_specs=[inside] * 3,
        out_specs=[anywhere] * len(shapes),
        scratch_shapes=[
            pltpu.VMEM((N, W + N), f32),
            pltpu.VMEM((NZ, 2, W + 8, N), f32),
            pltpu.VMEM((4, 4, 64, K), f32),
            pltpu.VMEM((4, 4, 32, K), f32),
            pltpu.VMEM((8, PANEL), f32),
            pltpu.VMEM((NZ, W, 256), bf16),
            pltpu.VMEM((NZ, W, 256), bf16),
            pltpu.VMEM((W, K), bf16),
            pltpu.VMEM((W, K), bf16),
            pltpu.VMEM((PANEL, K), bf16),
            pltpu.VMEM((PANEL, K), bf16),
            pltpu.VMEM((W, W), f32),
            pltpu.VMEM((W, PANEL), f32),
            pltpu.VMEM((PANEL, W), f32),
            pltpu.VMEM((PANEL, PANEL), f32),
            pltpu.VMEM((8, W), f32),
            pltpu.VMEM((8, PANEL), f32),
            dma, dma, dma, dma,
            dma((2, 4, 2)), dma((2, 4, 2)),
            dma((16,)), dma((16,)),
            dma((16,)), dma((2,)),
            dma((16,)), dma,
            dma((7,)), dma((7,)),
            dma((2, 20)), dma((2, 20)),
            dma, dma,
            dma((7,)), dma((7,)), dma((7,)),
        ],
        compiler_params=pltpu.CompilerParams(
            collective_id=0, has_side_effects=True, vmem_limit_bytes=58 << 20
        ),
        name="gather",
    )(samples, targets, ridge)


def finish_kernel(tpre, gi0, g0j, g00, rhs, top, ridge0, ridge, out, panel, reduced, a, m, ab, mm, pj):
    i, j = lax.axis_index("gr"), lax.axis_index("gc")
    scale = 1.0 / K
    a[...] = g00[...]
    factor_inverse(a, m, ab, mm)
    across, along = ((1,), (1,)), ((1,), (0,))

    def diagonal(shape, value):
        row = lax.broadcasted_iota(jnp.int32, shape, 0)
        col = lax.broadcasted_iota(jnp.int32, shape, 1)
        return jnp.where(row == col, value, 0.0)

    on_i = jnp.where(i == 0, 1.0, 0.0)
    on_j = jnp.where(j == 0, 1.0, 0.0)
    on_ij = jnp.where(i == j, 1.0, 0.0)
    square = (PANEL, PANEL)
    for b in range(2):
        rows = slice(b * PANEL, (b + 1) * PANEL)
        left, right = gi0[rows, :] * scale, g0j[:, rows] * scale
        if b == 0:
            left = left + diagonal(square, ridge0[0:1, :] * on_i)
            right = right + diagonal(square, ridge0[0:1, :] * on_j)
        panel[rows, :] = dot3(left, m[...], across)
        pj[:, rows] = dot3(m[...], right, along)
    for b in range(2):
        cols = slice(b * PANEL, (b + 1) * PANEL)
        for c in range(2):
            rows = slice(c * PANEL, (c + 1) * PANEL)
            tile = tpre[rows, cols] * scale - dot3(panel[rows, :], pj[:, cols], along)
            if b == c:
                tile = tile + diagonal(square, ridge[0:1, cols] * on_ij)
            out[rows, cols] = tile
    solved = fdot(top[...] * scale, m[...], across)
    reduced[...] = rhs[...] * scale - fdot(solved, panel[...], across)


def finish(tpre, gi0, g0j, g00, rhs, top, ridge0, ridge):
    inside = pl.BlockSpec(memory_space=pltpu.VMEM)
    return pl.pallas_call(
        finish_kernel,
        out_shape=[
            jax.ShapeDtypeStruct((W, W), f32),
            jax.ShapeDtypeStruct((W, PANEL), f32),
            jax.ShapeDtypeStruct((8, W), f32),
        ],
        in_specs=[inside] * 8,
        out_specs=[inside] * 3,
        scratch_shapes=[
            pltpu.VMEM((PANEL, PANEL), f32),
            pltpu.VMEM((PANEL, PANEL), f32),
            pltpu.VMEM((N, 2 * N), f32),
            pltpu.VMEM((N, N), f32),
            pltpu.VMEM((PANEL, W), f32),
        ],
        compiler_params=pltpu.CompilerParams(vmem_limit_bytes=50 << 20),
        name="finish",
    )(tpre, gi0, g0j, g00, rhs, top, ridge0, ridge)


def on_device(samples, targets, ridge):
    targets = jnp.broadcast_to(targets[:, None], (targets.shape[0], N))
    ridge = jnp.broadcast_to(ridge[None, :], (8, ridge.shape[0]))
    trailing, panel, reduced = finish(*gather(samples, targets, ridge), ridge)
    return trailing, panel, reduced[0]


def solution(mesh):
    in_specs = (P(("rows", "gc"), "gr"), P(("rows", "gc")), P("gr"))
    out_specs = (P("gr", "gc"), P("gr", None), P("gr"))
    return jax.shard_map(on_device, mesh=mesh, in_specs=in_specs, out_specs=out_specs, check_vma=False)
```

```python
import jax
import jax.numpy as jnp
from jax import lax
from jax.experimental import pallas as pl
from jax.experimental.pallas import tpu as pltpu
from jax.sharding import PartitionSpec as P

f32, bf16 = jnp.float32, jnp.bfloat16
MESH = pl.DeviceIdType.MESH
PANEL = 512
W = 1024
K = 2048
NZ = 8
N = 128
Q = 256
NS = 3


def fdot(a, b, dims=((1,), (0,))):
    return lax.dot_general(a, b, (dims, ((), ())), precision=lax.Precision.HIGHEST, preferred_element_type=f32)


def bdot(a, b, dims=((1,), (0,))):
    return lax.dot_general(a, b, (dims, ((), ())), preferred_element_type=f32)


def high_low(x):
    high = x.astype(bf16)
    return high, (x - high.astype(f32)).astype(bf16)


def split3(x):
    a = x.astype(bf16).astype(f32)
    r = x - a
    b = r.astype(bf16).astype(f32)
    return a, b, r - b


def stack_left(x):
    a, b, c = split3(x)
    return jnp.concatenate([a, a, a, b, b, c], 0).astype(bf16)


def stack_right(x):
    a, b, c = split3(x)
    return jnp.concatenate([a, b, c, a, b, a], 0).astype(bf16)


def dot3(a, b, dims):
    (da,), (db,) = dims
    ah, al = high_low(a)
    bh, bl = high_low(b)
    return bdot(jnp.concatenate([ah, al, ah], da), jnp.concatenate([bh, bh, bl], db), dims)


def row_of(x, i):
    return jnp.broadcast_to(x[i : i + 1, :], (8, x.shape[1]))


def twice(x):
    return jnp.concatenate([x, x], 1)


def strip_factor(s, strip):
    left = strip[:, :N]
    cols = [jnp.take_along_axis(left, jnp.full((8, N), s * 8 + j, jnp.int32), axis=1) for j in range(8)]
    e = {(i, j): row_of(cols[j], i) for j in range(8) for i in range(j, 8)}
    t = [row_of(strip, i) for i in range(8)]
    f, inv, root = {}, [], []
    for k in range(8):
        r = lax.rsqrt(e[k, k])
        r = r * (1.5 - 0.5 * e[k, k] * r * r)
        p = r * r
        p = p * (2.0 - e[k, k] * p)
        inv.append(p)
        root.append(r)
        for i in range(k + 1, 8):
            f[i, k] = e[i, k] * p
        for j in range(k + 1, 8):
            for i in range(j, 8):
                e[i, j] = e[i, j] - f[i, k] * e[j, k]
        for i in range(k + 1, 8):
            t[i] = t[i] - twice(f[i, k]) * t[k]
    y = [None] * 8
    for i in reversed(range(8)):
        acc = t[i] * twice(inv[i])
        for k in range(i + 1, 8):
            acc = acc - twice(f[k, i]) * y[k]
        y[i] = acc
    row = lax.broadcasted_iota(jnp.int32, (8, N), 0)

    def assemble(parts):
        out = parts[0]
        rows = row if out.shape[1] == N else twice(row)
        for i in range(1, 8):
            out = jnp.where(rows == i, parts[i], out)
        return out

    return assemble(y), assemble([t[i][:, N:] * root[i] for i in range(8)]), y


def factor_block(ab, m_ref):
    def body(s, carry):
        strip, left, right = carry
        ab[...] = ab[...] - bdot(left, right)
        whole, inverse_rows, y = strip_factor(s, strip)
        m_ref[pl.ds(pl.multiple_of(s * 8, 8), 8), :] = inverse_rows
        after = lax.rem(s + 1, 16)
        rows = ab[pl.ds(pl.multiple_of(after * 8, 8), 8), :]
        terms = []
        for j in range(8):
            c = jnp.take_along_axis(rows[:, :N], jnp.full((8, N), s * 8 + j, jnp.int32), axis=1)
            terms.append(twice(c) * y[j])
        while len(terms) > 1:
            terms = [terms[i] + terms[i + 1] for i in range(0, len(terms), 2)]
        return rows - terms[0], stack_left(strip[:, :N]).T, stack_right(whole)

    lax.fori_loop(0, 16, body, (ab[0:8, :], jnp.zeros((N, 48), bf16), jnp.zeros((48, 2 * N), bf16)))


def factor_inverse(a, b, ab, m):
    b[...] = jnp.zeros_like(b)
    eye = jnp.where(
        lax.broadcasted_iota(jnp.int32, (N, N), 0) == lax.broadcasted_iota(jnp.int32, (N, N), 1), 1.0, 0.0
    )
    blocks = PANEL // N
    for k in range(blocks):
        now, rest = slice(k * N, (k + 1) * N), slice((k + 1) * N, PANEL)
        ab[:, :N] = a[now, now]
        ab[:, N:] = eye
        factor_block(ab, m)
        b[now, now] = m[...]
        if k:
            b[now, : k * N] = fdot(m[...], b[now, : k * N])
        if k < blocks - 1:
            u = fdot(m[...], a[now, rest])
            a[rest, rest] = a[rest, rest] - fdot(u, u, ((0,), (0,)))
            b[rest, : (k + 1) * N] = b[rest, : (k + 1) * N] - fdot(u, b[now, : (k + 1) * N], ((0,), (0,)))


def kernel(
    samp, targ, ridge,
    out_o, panel_o, red_o,
    chunk, ai, sj, zb, stage, rg, azh, azl, tg, gi0, acc, g00, inverse, ab, mm, panel, rhs, top, red,
    ex_s, ex_r, ye_s, ye_r, si_s, si_r, sc_s, sc_r, zs_s, zs_r, rg_s, rg_r, zz_s, zz_r, ag_s, ag_r, h_s, h_r, lo,
):
    r, i, z = lax.axis_index("rows"), lax.axis_index("gr"), lax.axis_index("gc")
    core, yl = lax.rem(r, 2), r // 2
    x, yh = i // 2, lax.rem(i, 2)
    y = yh * 2 + yl
    p = y * 4 + x
    first, second = core == 0, core == 1
    scale = 1.0 / K
    across, along = ((1,), (1,)), ((1,), (0,))

    def dev(xx, yy, zz, c):
        return {"rows": lax.rem(yy, 2) * 2 + c, "gr": xx * 2 + yy // 2, "gc": zz}

    def up(v, n):
        return lax.rem(v + 1, n)

    def down(v, n):
        return lax.rem(v + n - 1, n)

    sibling = dev(x, y, z, 1 - core)

    barrier = pltpu.get_barrier_semaphore()

    def greet(device):
        pl.semaphore_signal(barrier, inc=1, device_id=device, device_id_type=MESH)

    greet(sibling)
    for d in range(1, NZ):
        greet(dev(x, y, lax.rem(z + d, NZ), core))
    source = jnp.where(i == 0, 1, 0)

    @pl.when(second)
    def _():
        for d in range(1, 16):
            pp = lax.rem(p + d, 16)
            greet(dev(lax.rem(pp, 4), pp // 4, z, 1))
        pl.semaphore_wait(barrier, 23)

    @pl.when(first)
    def _():
        for xx, yy in ((up(x, 4), y), (down(x, 4), y), (x, up(y, 4)), (x, down(y, 4))):
            greet(dev(xx, yy, z, 0))
        for b in range(2):

            @pl.when(jnp.logical_not(jnp.logical_and(i == 0, yl == b)))
            def _():
                greet({"rows": b * 2, "gr": 0, "gc": z})

        pl.semaphore_wait(barrier, 12 + 15 * source)

    mine = pl.ds(pl.multiple_of(core * 64, 64), 64)
    theirs = pl.ds(pl.multiple_of((1 - core) * 64, 64), 64)
    chunk[mine, :W] = samp[...]
    chunk[mine, W:] = targ[...]
    swap = pltpu.make_async_remote_copy(
        chunk.at[mine], chunk.at[mine], ex_s, ex_r, device_id=sibling, device_id_type=MESH
    )
    swap.start()
    pltpu.make_async_remote_copy(
        chunk.at[theirs], chunk.at[theirs], ex_s, ex_r, device_id=sibling, device_id_type=MESH
    ).wait_recv()
    own = ai.at[z, yl]
    for b in range(W // N):
        own[b * N : (b + 1) * N, :] = chunk[:, b * N : (b + 1) * N].T
    own[W : W + 8, :] = chunk[:, W:].T[:8]

    def pair_lanes(zz):
        return pl.ds(pl.multiple_of(zz * 2 * N, 2 * N), 2 * N)

    def lanes(zz, b):
        return pl.ds(pl.multiple_of((zz * 2 + b) * N, N), N)

    def plane(buf, c, half_rows):
        sub = half_rows // 2

        def move(h, index, u_off, v_off, off, size, du, dv):
            a, b = (x, y) if h == 0 else (y, x)
            uu, vv = lax.rem(a + u_off + 4, 4), lax.rem(b + v_off + 4, 4)
            tu, tv = lax.rem(a + du + 4, 4), lax.rem(b + dv + 4, 4)
            rows = pl.ds(h * half_rows + off, size)
            item = buf.at[vv, uu, rows] if h == 0 else buf.at[uu, vv, rows]
            to = dev(tu, tv, z, c) if h == 0 else dev(tv, tu, z, c)
            return pltpu.make_async_remote_copy(
                item, item, ag_s.at[h, index], ag_r.at[h, index], device_id=to, device_id_type=MESH
            )

        offsets = (0, -1, 1, 2)

        def u_send(h, n):
            return (
                lambda: move(h, 0, 0, 0, 0, half_rows, 1, 0),
                lambda: move(h, 1, 0, 0, 0, half_rows, -1, 0),
                lambda: move(h, 2, -1, 0, 0, sub, 1, 0),
                lambda: move(h, 3, 1, 0, sub, sub, -1, 0),
            )[n]()

        def u_recv(h, n):
            return (
                lambda: move(h, 0, -1, 0, 0, half_rows, 1, 0),
                lambda: move(h, 1, 1, 0, 0, half_rows, -1, 0),
                lambda: move(h, 2, -2, 0, 0, sub, 1, 0),
                lambda: move(h, 3, 2, 0, sub, sub, -1, 0),
            )[n]()

        def v_send(h, o, n):
            at, u = 4 + 4 * o, offsets[o]
            return (
                lambda: move(h, at, u, 0, 0, half_rows, 0, 1),
                lambda: move(h, at + 1, u, 0, 0, half_rows, 0, -1),
                lambda: move(h, at + 2, u, -1, 0, sub, 0, 1),
                lambda: move(h, at + 3, u, 1, sub, sub, 0, -1),
            )[n]()

        def v_recv(h, o, n):
            at, u = 4 + 4 * o, offsets[o]
            return (
                lambda: move(h, at, u, -1, 0, half_rows, 0, 1),
                lambda: move(h, at + 1, u, 1, 0, half_rows, 0, -1),
                lambda: move(h, at + 2, u, -2, 0, sub, 0, 1),
                lambda: move(h, at + 3, u, 2, sub, sub, 0, -1),
            )[n]()

        def both(step):
            def run():
                for h in range(2):
                    step(h)

            return run

        def begin(h):
            u_send(h, 0).start()
            u_send(h, 1).start()
            v_send(h, 0, 0).start()
            v_send(h, 0, 1).start()

        def u_first(h):
            for n in range(2):
                u_recv(h, n).wait_recv()
                u_send(h, n + 2).start()
                v_send(h, n + 1, 0).start()
                v_send(h, n + 1, 1).start()

        def v_forward(o):
            def step(h):
                for n in range(2):
                    v_recv(h, o, n).wait_recv()
                    v_send(h, o, n + 2).start()

            return step

        def u_second(h):
            u_recv(h, 2).wait_recv()
            u_recv(h, 3).wait_recv()
            v_send(h, 3, 0).start()
            v_send(h, 3, 1).start()

        def end(h):
            for o in range(4):
                v_recv(h, o, 2).wait_recv()
                v_recv(h, o, 3).wait_recv()

        def sent(h):
            for n in range(4):
                u_send(h, n).wait_send()
                for o in range(4):
                    v_send(h, o, n).wait_send()

        return [both(s) for s in (begin, u_first, v_forward(0), u_second, v_forward(1), v_forward(2), v_forward(3), end, sent)]

    def give(n, src, dst):
        return pltpu.make_async_remote_copy(
            src, dst, h_s.at[n], h_r.at[n], device_id=sibling, device_id_type=MESH
        )

    def part(n):
        return pl.ds(pl.multiple_of(n * Q, Q), Q)

    give_gi0 = give(0, gi0, gi0)
    give_rhs = give(1, rhs, rhs)
    give_top = give(2, top, top)
    give_z = give(7, zb, zb)
    give_inverse = give(8, inverse, inverse)
    give_panel = give(9, panel, panel)
    give_red = give(10, red, red_o)
    keep_panel = pltpu.make_async_copy(panel, panel_o, lo.at[4])
    keep_red = pltpu.make_async_copy(red, red_o, lo.at[5])

    def give_tile(n):
        return give(3 + n, tg.at[:, part(n)], tg.at[:, part(n)])

    def give_out(n):
        return give(11 + n, tg.at[pl.ds(0, W), part(n)], out_o.at[:, part(n)])

    def keep_out(n):
        return pltpu.make_async_copy(tg.at[pl.ds(0, W), part(n)], out_o.at[:, part(n)], lo.at[n])

    def diagonal(shape, shift, value):
        row = lax.broadcasted_iota(jnp.int32, shape, 0)
        col = lax.broadcasted_iota(jnp.int32, shape, 1)
        return jnp.where(row == col + shift, value, 0.0)

    on_i = jnp.where(i == 0, 1.0, 0.0)
    on_j = jnp.where(z == 0, 1.0, 0.0)
    on_ij = jnp.where(i == z, 1.0, 0.0)

    def update(n):
        right = tg[W:, part(n)] * scale
        if n < 2:
            right = right + diagonal((PANEL, Q), n * Q, rg[0:1, n * Q : (n + 1) * Q] * on_j)
        column_factor = dot3(inverse[...], right, along)
        tile = tg[:W, part(n)] * scale - dot3(panel[...], column_factor, along)
        tg[:W, part(n)] = tile + diagonal((W, Q), n * Q, ridge[0:1, n * Q : (n + 1) * Q] * on_ij)
        keep_out(n).start()
        give_out(n).start()

    @pl.when(first)
    def _():
        def z_piece(d):
            pp = lax.rem(p + d, 16)
            return pltpu.make_async_remote_copy(
                own.at[pl.ds(pl.multiple_of(pp * 32, 32), 32)],
                zb.at[pp // 4, lax.rem(pp, 4), :, lanes(z, yl)],
                zs_s.at[d], zs_r.at[yl],
                device_id=dev(lax.rem(pp, 4), pp // 4, z, 0), device_id_type=MESH,
            )

        def r_piece(d):
            pp = lax.rem(p + d, 16)
            return pltpu.make_async_remote_copy(
                rg, rg, rg_s.at[d], rg_r, device_id=dev(lax.rem(pp, 4), pp // 4, z, 0), device_id_type=MESH
            )

        @pl.when(i == 0)
        def _():
            pltpu.make_async_copy(
                own.at[pl.ds(pl.multiple_of(p * 32, 32), 32)], zb.at[y, x, :, lanes(z, yl)], zs_r.at[yl]
            ).start()
            for d in range(1, 16):
                z_piece(d).start()

            @pl.when(yl == 0)
            def _():
                rg[...] = ridge[:, :PANEL]
                for d in range(1, 16):
                    r_piece(d).start()

        for b in range(2):
            at = zb.at[y, x, :, lanes(z, b)]
            pltpu.make_async_copy(at, at, zs_r.at[b]).wait()

        def z_plane(d):
            item = zb.at[y, x, :, pair_lanes(z)]
            return pltpu.make_async_remote_copy(
                item, item, zz_s.at[d - 1], zz_r.at[d - 1],
                device_id=dev(x, y, lax.rem(z + d, NZ), 0), device_id_type=MESH,
            )

        for d in (1, 7, 2, 6, 3, 5, 4):
            z_plane(d).start()
        for d in (1, 7, 2, 6, 3, 5, 4):
            item = zb.at[y, x, :, pair_lanes(lax.rem(z - d + NZ, NZ))]
            pltpu.make_async_remote_copy(
                item, item, zz_s.at[d - 1], zz_r.at[d - 1], device_id=sibling, device_id_type=MESH
            ).wait_recv()
        steps = plane(zb, 0, 16)
        for step in steps[:-1]:
            step()
        give_z.start()

        for b in range(2):
            rows = zb[b * 2 : b * 2 + 2].reshape(256, K)
            g00[b * 256 : (b + 1) * 256, :] = fdot(rows, zb[...].reshape(PANEL, K), across) * scale

        @pl.when(jnp.logical_not(jnp.logical_and(i == 0, yl == 0)))
        def _():
            r_piece(1).wait_recv()

        g00[...] = g00[...] + diagonal((PANEL, PANEL), 0, rg[0:1, :])
        factor_inverse(g00, inverse, ab, mm)
        give_inverse.start()

        give_gi0.wait_recv()
        for b in range(2):
            rows = slice(b * PANEL, (b + 1) * PANEL)
            panel[rows, :] = dot3(gi0[rows, :], inverse[...], across)
        give_panel.start()
        keep_panel.start()
        for n in range(NS):
            give_tile(n).wait_recv()
            update(n)
        give_rhs.wait_recv()
        give_top.wait_recv()
        solved = fdot(top[...], inverse[...], across)
        red[...] = rhs[...] - fdot(solved, panel[...], across)
        give_red.start()
        keep_red.start()

        steps[-1]()
        for d in range(1, NZ):
            z_plane(d).wait_send()

        @pl.when(i == 0)
        def _():
            for d in range(1, 16):
                z_piece(d).wait_send()

            @pl.when(yl == 0)
            def _():
                for d in range(1, 16):
                    r_piece(d).wait_send()

        give_z.wait_send()
        give_inverse.wait_send()
        give_panel.wait_send()
        give_red.wait_send()
        keep_panel.wait()
        keep_red.wait()
        for n in range(NS):
            keep_out(n).wait()
            give_out(n).wait_send()
        for n in range(NS, 4):
            give_out(n).wait_recv()

    @pl.when(second)
    def _():
        def ring(way, s, b):
            at = lax.rem(z - s + 1 + NZ, NZ) if way == 0 else lax.rem(z + s - 1, NZ)
            item = ai.at[at, yl if b == 0 else 1 - yl]
            to = dev(x, y, up(z, NZ) if way == 0 else down(z, NZ), 1)
            return pltpu.make_async_remote_copy(
                item, item, si_s.at[way, s - 1, b], si_r.at[way, s - 1, b], device_id=to, device_id_type=MESH
            )

        def ring_in(way, s, b):
            at = lax.rem(z - s + NZ, NZ) if way == 0 else lax.rem(z + s, NZ)
            item = ai.at[at, yl if b == 0 else 1 - yl]
            return pltpu.make_async_remote_copy(
                item, item, si_s.at[way, s - 1, b], si_r.at[way, s - 1, b], device_id=sibling, device_id_type=MESH
            )

        ring_list = [(s, b, way) for s in (1, 2, 3) for b in range(2) for way in range(2)] + [(4, 0, 0), (4, 1, 1)]

        def s_piece(d):
            pp = lax.rem(p + d, 16)
            return pltpu.make_async_remote_copy(
                own.at[pl.ds(pl.multiple_of(pp * 64, 64), 64)],
                stage.at[i, :, pl.ds(pl.multiple_of(yl * N, N), N)],
                sc_s.at[d], sc_r.at[i * 2 + yl],
                device_id=dev(lax.rem(pp, 4), pp // 4, z, 1), device_id_type=MESH,
            )

        for d in range(1, 16):
            s_piece(d).start()
        pltpu.make_async_copy(
            own.at[pl.ds(pl.multiple_of(p * 64, 64), 64)],
            stage.at[i, :, pl.ds(pl.multiple_of(yl * N, N), N)],
            sc_r.at[i * 2 + yl],
        ).start()
        partner = dev(x, yh * 2 + 1 - yl, z, 1)
        trade = pltpu.make_async_remote_copy(own, own, ye_s, ye_r, device_id=partner, device_id_type=MESH)
        trade.start()
        ring(0, 1, 0).start()
        ring(1, 1, 0).start()
        for n in range(16):
            at = stage.at[n // 2, :, pl.ds((n % 2) * N, N)]
            pltpu.make_async_copy(at, at, sc_r.at[n]).wait()

        def s_plane(d):
            to = lax.rem(z + d, NZ)
            return pltpu.make_async_remote_copy(
                stage.at[to], sj.at[y, x, :, pair_lanes(z)], zz_s.at[d - 1], zz_r.at[d - 1],
                device_id=dev(x, y, to, 1), device_id_type=MESH,
            )

        for d in (1, 7, 2, 6, 3, 5, 4):
            s_plane(d).start()
        stay = pltpu.make_async_copy(stage.at[z], sj.at[y, x, :, pair_lanes(z)], lo.at[6])
        stay.start()
        other = ai.at[z, 1 - yl]
        pltpu.make_async_remote_copy(other, other, ye_s, ye_r, device_id=partner, device_id_type=MESH).wait_recv()
        ring(0, 1, 1).start()
        ring(1, 1, 1).start()
        for d in (1, 7, 2, 6, 3, 5, 4):
            item = sj.at[y, x, :, pair_lanes(lax.rem(z - d + NZ, NZ))]
            pltpu.make_async_remote_copy(
                item, item, zz_s.at[d - 1], zz_r.at[d - 1], device_id=sibling, device_id_type=MESH
            ).wait_recv()
        stay.wait()
        steps = plane(sj, 1, 32)

        def advance(s, b, way):
            ring_in(way, s, b).wait_recv()
            if (s + 1, b, way) in ring_list:
                ring(way, s + 1, b).start()

        moves = list(ring_list)
        steps[0]()
        for step in steps[1:-1]:
            if len(moves) > 2:
                advance(*moves.pop(0))
                advance(*moves.pop(0))
            step()
        give_z.wait_recv()

        def group(offsets, fresh):
            items = [lax.rem(z + o + NZ, NZ) for o in offsets]

            def put(ref, index, value):
                if fresh:
                    ref[index] = value
                else:
                    ref[index] += value

            def target(it, b):
                return ai[it, b, W : W + 1, :]

            def split_rows(n, c):
                rows = pl.ds(pl.multiple_of(n * N, N), N)
                total = jnp.zeros((N, N), f32)
                for slot, it in enumerate(items):
                    for b in range(2):
                        v = ai[it, b, rows, :]
                        h, l = high_low(v)
                        azh[slot, rows, b * N : (b + 1) * N] = h
                        azl[slot, rows, b * N : (b + 1) * N] = l
                        total = total + v * target(it, b)
                put(acc, (rows, slice(None)), total)
                return c

            lax.fori_loop(0, W // N, split_rows, 0)

            def split_leading(n, c):
                rows = pl.ds(pl.multiple_of(W + n * N, N), N)
                total = jnp.zeros((N, N), f32)
                for slot, it in enumerate(items):
                    v = zb[n, :, :, pair_lanes(it)].reshape(N, 2 * N)
                    h, l = high_low(v)
                    azh[slot, rows, :] = h
                    azl[slot, rows, :] = l
                    for b in range(2):
                        total = total + v[:, b * N : (b + 1) * N] * target(it, b)
                put(acc, (rows, slice(None)), total)
                return c

            lax.fori_loop(0, PANEL // N, split_leading, 0)

            def left(rows):
                parts = []
                for slot in range(4):
                    h, l = azh[slot, rows, :], azl[slot, rows, :]
                    parts += [h, l, h]
                return jnp.concatenate(parts, 1)

            def panel_columns(n, c):
                rows = pl.ds(pl.multiple_of(W + n * Q, Q), Q)
                parts = []
                for slot in range(4):
                    h, l = azh[slot, rows, :], azl[slot, rows, :]
                    parts += [h, h, l]
                put(gi0, (slice(None), part(n)), bdot(left(pl.ds(0, W)), jnp.concatenate(parts, 1), across))
                return c

            lax.fori_loop(0, PANEL // Q, panel_columns, 0)
            if not fresh:
                gi0[...] = gi0[...] * scale
                gi0[:PANEL, :] += diagonal((PANEL, PANEL), 0, ridge[0:1, :PANEL] * on_i)
                give_gi0.start()

            def columns(n, c):
                parts = []
                for it in items:
                    h, l = high_low(sj[n, :, :, pair_lanes(it)].reshape(Q, 2 * N))
                    parts += [h, h, l]
                put(tg, (slice(None), part(n)), bdot(left(pl.ds(0, W + PANEL)), jnp.concatenate(parts, 1), across))
                if not fresh:

                    @pl.when(n < NS)
                    def _():
                        give_tile(n).start()

                return c

            lax.fori_loop(0, 4, columns, 0)

        group((0, -1, 1, -2), True)
        while moves:
            advance(*moves.pop(0))
        group((2, -3, 3, 4), False)
        ones = jnp.full((8, N), scale, f32)
        rhs[...] = fdot(ones, acc[:W, :], across)
        top[...] = fdot(ones, acc[W:, :], across)
        give_rhs.start()
        give_top.start()
        give_inverse.wait_recv()
        give_panel.wait_recv()
        keep_panel.start()
        for n in range(NS, 4):
            update(n)

        steps[-1]()
        for s, b, way in ring_list:
            ring(way, s, b).wait_send()
        trade.wait_send()
        for d in range(1, 16):
            s_piece(d).wait_send()
        for d in range(1, NZ):
            s_plane(d).wait_send()
        give_gi0.wait_send()
        give_rhs.wait_send()
        give_top.wait_send()
        keep_panel.wait()
        for n in range(NS):
            give_tile(n).wait_send()
            give_out(n).wait_recv()
        for n in range(NS, 4):
            keep_out(n).wait()
            give_out(n).wait_send()
        give_red.wait_recv()

    swap.wait_send()


def on_device(samples, targets, ridge):
    targets = jnp.broadcast_to(targets[:, None], (targets.shape[0], N))
    ridge = jnp.broadcast_to(ridge[None, :], (8, ridge.shape[0]))
    anywhere = pl.BlockSpec(memory_space=pl.ANY)
    inside = pl.BlockSpec(memory_space=pltpu.VMEM)
    dma = pltpu.SemaphoreType.DMA
    shapes = [(W, W), (W, PANEL), (8, W)]
    trailing, panel, reduced = pl.pallas_call(
        kernel,
        out_shape=[jax.ShapeDtypeStruct(s, f32) for s in shapes],
        in_specs=[inside] * 3,
        out_specs=[anywhere] * len(shapes),
        scratch_shapes=[
            pltpu.VMEM((N, W + N), f32),
            pltpu.VMEM((NZ, 2, W + 8, N), f32),
            pltpu.VMEM((4, 4, 64, K), f32),
            pltpu.VMEM((4, 4, 32, K), f32),
            pltpu.VMEM((NZ, 64, 2 * N), f32),
            pltpu.VMEM((8, PANEL), f32),
            pltpu.VMEM((4, W + PANEL, 2 * N), bf16),
            pltpu.VMEM((4, W + PANEL, 2 * N), bf16),
            pltpu.VMEM((W + PANEL, W), f32),
            pltpu.VMEM((W, PANEL), f32),
            pltpu.VMEM((W + PANEL, N), f32),
            pltpu.VMEM((PANEL, PANEL), f32),
            pltpu.VMEM((PANEL, PANEL), f32),
            pltpu.VMEM((N, 2 * N), f32),
            pltpu.VMEM((N, N), f32),
            pltpu.VMEM((W, PANEL), f32),
            pltpu.VMEM((8, W), f32),
            pltpu.VMEM((8, PANEL), f32),
            pltpu.VMEM((8, W), f32),
            dma, dma, dma, dma,
            dma((2, 4, 2)), dma((2, 4, 2)),
            dma((16,)), dma((16,)),
            dma((16,)), dma((2,)),
            dma((16,)), dma,
            dma((7,)), dma((7,)),
            dma((2, 20)), dma((2, 20)),
            dma((15,)), dma((15,)), dma((7,)),
        ],
        compiler_params=pltpu.CompilerParams(
            collective_id=0, has_side_effects=True, vmem_limit_bytes=56 << 20
        ),
        name="ridge_panel",
    )(samples, targets, ridge)
    return trailing, panel, reduced[0]


def solution(mesh):
    in_specs = (P(("rows", "gc"), "gr"), P(("rows", "gc")), P("gr"))
    out_specs = (P("gr", "gc"), P("gr", None), P("gr"))
    return jax.shard_map(on_device, mesh=mesh, in_specs=in_specs, out_specs=out_specs, check_vma=False)
```

```python
import jax
import jax.numpy as jnp
from jax import lax
from jax.experimental import pallas as pl
from jax.experimental.pallas import tpu as pltpu
from jax.sharding import PartitionSpec as P

f32, bf16 = jnp.float32, jnp.bfloat16
MESH = pl.DeviceIdType.MESH
PANEL = 512
W = 1024
K = 2048
NZ = 8
N = 128
Q = 256
NS = 2


def fdot(a, b, dims=((1,), (0,))):
    return lax.dot_general(a, b, (dims, ((), ())), precision=lax.Precision.HIGHEST, preferred_element_type=f32)


def bdot(a, b, dims=((1,), (0,))):
    return lax.dot_general(a, b, (dims, ((), ())), preferred_element_type=f32)


def high_low(x):
    high = x.astype(bf16)
    return high, (x - high.astype(f32)).astype(bf16)


def split3(x):
    a = x.astype(bf16).astype(f32)
    r = x - a
    b = r.astype(bf16).astype(f32)
    return a, b, r - b


def stack_left(x):
    a, b, c = split3(x)
    return jnp.concatenate([a, a, a, b, b, c], 0).astype(bf16)


def stack_right(x):
    a, b, c = split3(x)
    return jnp.concatenate([a, b, c, a, b, a], 0).astype(bf16)


def dot3(a, b, dims):
    (da,), (db,) = dims
    ah, al = high_low(a)
    bh, bl = high_low(b)
    return bdot(jnp.concatenate([ah, al, ah], da), jnp.concatenate([bh, bh, bl], db), dims)


def row_of(x, i):
    return jnp.broadcast_to(x[i : i + 1, :], (8, x.shape[1]))


def twice(x):
    return jnp.concatenate([x, x], 1)


def strip_factor(s, strip):
    left = strip[:, :N]
    cols = [jnp.take_along_axis(left, jnp.full((8, N), s * 8 + j, jnp.int32), axis=1) for j in range(8)]
    e = {(i, j): row_of(cols[j], i) for j in range(8) for i in range(j, 8)}
    t = [row_of(strip, i) for i in range(8)]
    f, inv, root = {}, [], []
    for k in range(8):
        r = lax.rsqrt(e[k, k])
        r = r * (1.5 - 0.5 * e[k, k] * r * r)
        p = r * r
        p = p * (2.0 - e[k, k] * p)
        inv.append(p)
        root.append(r)
        for i in range(k + 1, 8):
            f[i, k] = e[i, k] * p
        for j in range(k + 1, 8):
            for i in range(j, 8):
                e[i, j] = e[i, j] - f[i, k] * e[j, k]
        for i in range(k + 1, 8):
            t[i] = t[i] - twice(f[i, k]) * t[k]
    y = [None] * 8
    for i in reversed(range(8)):
        acc = t[i] * twice(inv[i])
        for k in range(i + 1, 8):
            acc = acc - twice(f[k, i]) * y[k]
        y[i] = acc
    row = lax.broadcasted_iota(jnp.int32, (8, N), 0)

    def assemble(parts):
        out = parts[0]
        rows = row if out.shape[1] == N else twice(row)
        for i in range(1, 8):
            out = jnp.where(rows == i, parts[i], out)
        return out

    return assemble(y), assemble([t[i][:, N:] * root[i] for i in range(8)]), y


def factor_block(ab, m_ref):
    def body(s, carry):
        strip, left, right = carry
        ab[...] = ab[...] - bdot(left, right)
        whole, inverse_rows, y = strip_factor(s, strip)
        m_ref[pl.ds(pl.multiple_of(s * 8, 8), 8), :] = inverse_rows
        after = lax.rem(s + 1, 16)
        rows = ab[pl.ds(pl.multiple_of(after * 8, 8), 8), :]
        terms = []
        for j in range(8):
            c = jnp.take_along_axis(rows[:, :N], jnp.full((8, N), s * 8 + j, jnp.int32), axis=1)
            terms.append(twice(c) * y[j])
        while len(terms) > 1:
            terms = [terms[i] + terms[i + 1] for i in range(0, len(terms), 2)]
        return rows - terms[0], stack_left(strip[:, :N]).T, stack_right(whole)

    lax.fori_loop(0, 16, body, (ab[0:8, :], jnp.zeros((N, 48), bf16), jnp.zeros((48, 2 * N), bf16)))


def factor_inverse(a, b, ab, m):
    b[...] = jnp.zeros_like(b)
    eye = jnp.where(
        lax.broadcasted_iota(jnp.int32, (N, N), 0) == lax.broadcasted_iota(jnp.int32, (N, N), 1), 1.0, 0.0
    )
    blocks = PANEL // N
    for k in range(blocks):
        now, rest = slice(k * N, (k + 1) * N), slice((k + 1) * N, PANEL)
        ab[:, :N] = a[now, now]
        ab[:, N:] = eye
        factor_block(ab, m)
        b[now, now] = m[...]
        if k:
            b[now, : k * N] = fdot(m[...], b[now, : k * N])
        if k < blocks - 1:
            u = fdot(m[...], a[now, rest])
            a[rest, rest] = a[rest, rest] - fdot(u, u, ((0,), (0,)))
            b[rest, : (k + 1) * N] = b[rest, : (k + 1) * N] - fdot(u, b[now, : (k + 1) * N], ((0,), (0,)))


def kernel(
    samp, targ, ridge,
    out_o, panel_o, red_o,
    chunk, tr, ai, sj, zb, stage, rg, azh, azl, tg, gi0, acc, g00, inverse, ab, mm, panel, rhs, top, red,
    ex_s, ex_r, ye_s, ye_r, si_s, si_r, sc_s, sc_r, zs_s, zs_r, rg_s, rg_r, zz_s, zz_r, ag_s, ag_r, h_s, h_r, lo,
):
    r, i, z = lax.axis_index("rows"), lax.axis_index("gr"), lax.axis_index("gc")
    core, yl = lax.rem(r, 2), r // 2
    x, yh = i // 2, lax.rem(i, 2)
    y = yh * 2 + yl
    p = y * 4 + x
    first, second = core == 0, core == 1
    scale = 1.0 / K
    across, along = ((1,), (1,)), ((1,), (0,))

    def dev(xx, yy, zz, c):
        return {"rows": lax.rem(yy, 2) * 2 + c, "gr": xx * 2 + yy // 2, "gc": zz}

    def up(v, n):
        return lax.rem(v + 1, n)

    def down(v, n):
        return lax.rem(v + n - 1, n)

    sibling = dev(x, y, z, 1 - core)

    barrier = pltpu.get_barrier_semaphore()

    def greet(device):
        pl.semaphore_signal(barrier, inc=1, device_id=device, device_id_type=MESH)

    greet(sibling)
    for d in range(1, NZ):
        greet(dev(x, y, lax.rem(z + d, NZ), core))
    source = jnp.where(i == 0, 1, 0)

    @pl.when(second)
    def _():
        for d in range(1, 16):
            pp = lax.rem(p + d, 16)
            greet(dev(lax.rem(pp, 4), pp // 4, z, 1))
        pl.semaphore_wait(barrier, 23)

    @pl.when(first)
    def _():
        for xx, yy in ((up(x, 4), y), (down(x, 4), y), (x, up(y, 4)), (x, down(y, 4))):
            greet(dev(xx, yy, z, 0))
        for b in range(2):

            @pl.when(jnp.logical_not(jnp.logical_and(i == 0, yl == b)))
            def _():
                greet({"rows": b * 2, "gr": 0, "gc": z})

        pl.semaphore_wait(barrier, 12 + 15 * source)

    mine = pl.ds(pl.multiple_of(core * 64, 64), 64)
    theirs = pl.ds(pl.multiple_of((1 - core) * 64, 64), 64)
    chunk[mine, :] = samp[...]
    tr[core, :, :64] = jnp.broadcast_to(targ[...], (8, 64))
    swap = pltpu.make_async_remote_copy(
        chunk.at[mine], chunk.at[mine], ex_s.at[0], ex_r.at[0], device_id=sibling, device_id_type=MESH
    )
    swap.start()
    swap_targets = pltpu.make_async_remote_copy(
        tr.at[core], tr.at[core], ex_s.at[1], ex_r.at[1], device_id=sibling, device_id_type=MESH
    )
    swap_targets.start()
    pltpu.make_async_remote_copy(
        chunk.at[theirs], chunk.at[theirs], ex_s.at[0], ex_r.at[0], device_id=sibling, device_id_type=MESH
    ).wait_recv()
    own = ai.at[z, yl]
    for b in range(W // N):
        own[b * N : (b + 1) * N, :] = chunk[:, b * N : (b + 1) * N].T
    pltpu.make_async_remote_copy(
        tr.at[1 - core], tr.at[1 - core], ex_s.at[1], ex_r.at[1], device_id=sibling, device_id_type=MESH
    ).wait_recv()
    lane = lax.broadcasted_iota(jnp.int32, (8, N), 1)
    own[W : W + 8, :] = jnp.where(lane < 64, tr[0], pltpu.roll(tr[1], 64, 1))

    def pair_lanes(zz):
        return pl.ds(pl.multiple_of(zz * 2 * N, 2 * N), 2 * N)

    def lanes(zz, b):
        return pl.ds(pl.multiple_of((zz * 2 + b) * N, N), N)

    def plane(buf, c, half_rows, pass_on=None):
        sub = half_rows // 2

        def arrived(copy):
            copy.wait_recv()
            if pass_on is not None:
                pass_on(copy.src_ref)


        def move(h, index, u_off, v_off, off, size, du, dv):
            a, b = (x, y) if h == 0 else (y, x)
            uu, vv = lax.rem(a + u_off + 4, 4), lax.rem(b + v_off + 4, 4)
            tu, tv = lax.rem(a + du + 4, 4), lax.rem(b + dv + 4, 4)
            rows = pl.ds(h * half_rows + off, size)
            item = buf.at[vv, uu, rows] if h == 0 else buf.at[uu, vv, rows]
            to = dev(tu, tv, z, c) if h == 0 else dev(tv, tu, z, c)
            return pltpu.make_async_remote_copy(
                item, item, ag_s.at[h, index], ag_r.at[h, index], device_id=to, device_id_type=MESH
            )

        offsets = (0, -1, 1, 2)

        def u_send(h, n):
            return (
                lambda: move(h, 0, 0, 0, 0, half_rows, 1, 0),
                lambda: move(h, 1, 0, 0, 0, half_rows, -1, 0),
                lambda: move(h, 2, -1, 0, 0, sub, 1, 0),
                lambda: move(h, 3, 1, 0, sub, sub, -1, 0),
            )[n]()

        def u_recv(h, n):
            return (
                lambda: move(h, 0, -1, 0, 0, half_rows, 1, 0),
                lambda: move(h, 1, 1, 0, 0, half_rows, -1, 0),
                lambda: move(h, 2, -2, 0, 0, sub, 1, 0),
                lambda: move(h, 3, 2, 0, sub, sub, -1, 0),
            )[n]()

        def v_send(h, o, n):
            at, u = 4 + 4 * o, offsets[o]
            return (
                lambda: move(h, at, u, 0, 0, half_rows, 0, 1),
                lambda: move(h, at + 1, u, 0, 0, half_rows, 0, -1),
                lambda: move(h, at + 2, u, -1, 0, sub, 0, 1),
                lambda: move(h, at + 3, u, 1, sub, sub, 0, -1),
            )[n]()

        def v_recv(h, o, n):
            at, u = 4 + 4 * o, offsets[o]
            return (
                lambda: move(h, at, u, -1, 0, half_rows, 0, 1),
                lambda: move(h, at + 1, u, 1, 0, half_rows, 0, -1),
                lambda: move(h, at + 2, u, -2, 0, sub, 0, 1),
                lambda: move(h, at + 3, u, 2, sub, sub, 0, -1),
            )[n]()

        def both(step):
            def run():
                for h in range(2):
                    step(h)

            return run

        def begin(h):
            first_copy = u_send(h, 0)
            first_copy.start()
            if pass_on is not None:
                pass_on(first_copy.src_ref)
            u_send(h, 1).start()
            v_send(h, 0, 0).start()
            v_send(h, 0, 1).start()

        def u_first(h):
            for n in range(2):
                arrived(u_recv(h, n))
                u_send(h, n + 2).start()
                v_send(h, n + 1, 0).start()
                v_send(h, n + 1, 1).start()

        def v_forward(o):
            def step(h):
                for n in range(2):
                    arrived(v_recv(h, o, n))
                    v_send(h, o, n + 2).start()

            return step

        def u_second(h):
            arrived(u_recv(h, 2))
            arrived(u_recv(h, 3))
            v_send(h, 3, 0).start()
            v_send(h, 3, 1).start()

        def end(h):
            for o in range(4):
                arrived(v_recv(h, o, 2))
                arrived(v_recv(h, o, 3))

        def sent(h):
            for n in range(4):
                u_send(h, n).wait_send()
                for o in range(4):
                    v_send(h, o, n).wait_send()

        return [both(s) for s in (begin, u_first, v_forward(0), u_second, v_forward(1), v_forward(2), v_forward(3), end, sent)]

    def give(n, src, dst):
        return pltpu.make_async_remote_copy(
            src, dst, h_s.at[n], h_r.at[n], device_id=sibling, device_id_type=MESH
        )

    def part(n):
        return pl.ds(pl.multiple_of(n * Q, Q), Q)

    give_gi0 = give(0, gi0, gi0)
    give_rhs = give(1, rhs, rhs)
    give_top = give(2, top, top)
    give_z = give(7, zb, zb)
    give_inverse = give(8, inverse, inverse)
    give_panel = give(9, panel, panel)
    give_red = give(10, red, red_o)
    keep_panel = pltpu.make_async_copy(panel, panel_o, lo.at[4])
    keep_red = pltpu.make_async_copy(red, red_o, lo.at[5])

    def give_tile(n):
        return give(3 + n, tg.at[:, part(n)], tg.at[:, part(n)])

    def give_out(n):
        return give(11 + n, tg.at[pl.ds(0, W), part(n)], out_o.at[:, part(n)])

    def keep_out(n):
        return pltpu.make_async_copy(tg.at[pl.ds(0, W), part(n)], out_o.at[:, part(n)], lo.at[n])

    def diagonal(shape, shift, value):
        row = lax.broadcasted_iota(jnp.int32, shape, 0)
        col = lax.broadcasted_iota(jnp.int32, shape, 1)
        return jnp.where(row == col + shift, value, 0.0)

    on_i = jnp.where(i == 0, 1.0, 0.0)
    on_j = jnp.where(z == 0, 1.0, 0.0)
    on_ij = jnp.where(i == z, 1.0, 0.0)

    def update(n):
        right = tg[W:, part(n)] * scale
        if n < 2:
            right = right + diagonal((PANEL, Q), n * Q, rg[0:1, n * Q : (n + 1) * Q] * on_j)
        column_factor = dot3(inverse[...], right, along)
        tile = tg[:W, part(n)] * scale - dot3(panel[...], column_factor, along)
        tg[:W, part(n)] = tile + diagonal((W, Q), n * Q, ridge[0:1, n * Q : (n + 1) * Q] * on_ij)
        keep_out(n).start()
        give_out(n).start()

    @pl.when(first)
    def _():
        def z_piece(d):
            pp = lax.rem(p + d, 16)
            return pltpu.make_async_remote_copy(
                own.at[pl.ds(pl.multiple_of(pp * 32, 32), 32)],
                zb.at[pp // 4, lax.rem(pp, 4), :, lanes(z, yl)],
                zs_s.at[d], zs_r.at[yl],
                device_id=dev(lax.rem(pp, 4), pp // 4, z, 0), device_id_type=MESH,
            )

        def r_piece(d):
            pp = lax.rem(p + d, 16)
            return pltpu.make_async_remote_copy(
                rg, rg, rg_s.at[d], rg_r, device_id=dev(lax.rem(pp, 4), pp // 4, z, 0), device_id_type=MESH
            )

        @pl.when(i == 0)
        def _():
            pltpu.make_async_copy(
                own.at[pl.ds(pl.multiple_of(p * 32, 32), 32)], zb.at[y, x, :, lanes(z, yl)], zs_r.at[yl]
            ).start()
            for d in range(1, 16):
                z_piece(d).start()

            @pl.when(yl == 0)
            def _():
                rg[...] = jnp.broadcast_to(ridge[:, :PANEL], (8, PANEL))
                for d in range(1, 16):
                    r_piece(d).start()

        for b in range(2):
            at = zb.at[y, x, :, lanes(z, b)]
            pltpu.make_async_copy(at, at, zs_r.at[b]).wait()

        def z_plane(d):
            item = zb.at[y, x, :, pair_lanes(z)]
            return pltpu.make_async_remote_copy(
                item, item, zz_s.at[d - 1], zz_r.at[d - 1],
                device_id=dev(x, y, lax.rem(z + d, NZ), 0), device_id_type=MESH,
            )

        for d in (1, 7, 2, 6, 3, 5, 4):
            z_plane(d).start()
        for d in (1, 7, 2, 6, 3, 5, 4):
            item = zb.at[y, x, :, pair_lanes(lax.rem(z - d + NZ, NZ))]
            pltpu.make_async_remote_copy(
                item, item, zz_s.at[d - 1], zz_r.at[d - 1], device_id=sibling, device_id_type=MESH
            ).wait_recv()
        steps = plane(zb, 0, 16, lambda item: give(7, item, item).start())
        for step in steps[:-1]:
            step()

        for b in range(2):
            rows = zb[b * 2 : b * 2 + 2].reshape(256, K)
            g00[b * 256 : (b + 1) * 256, :] = fdot(rows, zb[...].reshape(PANEL, K), across) * scale

        @pl.when(jnp.logical_not(jnp.logical_and(i == 0, yl == 0)))
        def _():
            r_piece(1).wait_recv()

        g00[...] = g00[...] + diagonal((PANEL, PANEL), 0, rg[0:1, :])
        factor_inverse(g00, inverse, ab, mm)
        give_inverse.start()

        give_gi0.wait_recv()
        for b in range(2):
            rows = slice(b * PANEL, (b + 1) * PANEL)
            panel[rows, :] = dot3(gi0[rows, :], inverse[...], across)
        give_panel.start()
        keep_panel.start()
        for n in range(NS):
            give_tile(n).wait_recv()
            update(n)
        give_rhs.wait_recv()
        give_top.wait_recv()
        solved = fdot(top[...], inverse[...], across)
        red[...] = (rhs[...] - fdot(solved, panel[...], across))[:1]
        give_red.start()
        keep_red.start()

        steps[-1]()
        for d in range(1, NZ):
            z_plane(d).wait_send()

        @pl.when(i == 0)
        def _():
            for d in range(1, 16):
                z_piece(d).wait_send()

            @pl.when(yl == 0)
            def _():
                for d in range(1, 16):
                    r_piece(d).wait_send()

        give_z.wait_send()
        give_inverse.wait_send()
        give_panel.wait_send()
        give_red.wait_send()
        keep_panel.wait()
        keep_red.wait()
        for n in range(NS):
            keep_out(n).wait()
            give_out(n).wait_send()
        for n in range(NS, 4):
            give_out(n).wait_recv()

    @pl.when(second)
    def _():
        def ring(way, s, b):
            at = lax.rem(z - s + 1 + NZ, NZ) if way == 0 else lax.rem(z + s - 1, NZ)
            item = ai.at[at, yl if b == 0 else 1 - yl]
            to = dev(x, y, up(z, NZ) if way == 0 else down(z, NZ), 1)
            return pltpu.make_async_remote_copy(
                item, item, si_s.at[way, s - 1, b], si_r.at[way, s - 1, b], device_id=to, device_id_type=MESH
            )

        def ring_in(way, s, b):
            at = lax.rem(z - s + NZ, NZ) if way == 0 else lax.rem(z + s, NZ)
            item = ai.at[at, yl if b == 0 else 1 - yl]
            return pltpu.make_async_remote_copy(
                item, item, si_s.at[way, s - 1, b], si_r.at[way, s - 1, b], device_id=sibling, device_id_type=MESH
            )

        ring_list = [(s, b, way) for s in (1, 2, 3) for b in range(2) for way in range(2)] + [(4, 0, 0), (4, 1, 1)]

        def s_piece(d):
            pp = lax.rem(p + d, 16)
            return pltpu.make_async_remote_copy(
                own.at[pl.ds(pl.multiple_of(pp * 64, 64), 64)],
                stage.at[i, :, pl.ds(pl.multiple_of(yl * N, N), N)],
                sc_s.at[d], sc_r.at[i * 2 + yl],
                device_id=dev(lax.rem(pp, 4), pp // 4, z, 1), device_id_type=MESH,
            )

        for d in range(1, 16):
            s_piece(d).start()
        pltpu.make_async_copy(
            own.at[pl.ds(pl.multiple_of(p * 64, 64), 64)],
            stage.at[i, :, pl.ds(pl.multiple_of(yl * N, N), N)],
            sc_r.at[i * 2 + yl],
        ).start()
        partner = dev(x, yh * 2 + 1 - yl, z, 1)
        trade = pltpu.make_async_remote_copy(own, own, ye_s, ye_r, device_id=partner, device_id_type=MESH)
        trade.start()
        ring(0, 1, 0).start()
        ring(1, 1, 0).start()

        def staged(gr):
            for b in range(2):
                at = stage.at[gr, :, pl.ds(b * N, N)]
                pltpu.make_async_copy(at, at, sc_r.at[gr * 2 + b]).wait()

        def advance(s, b, way):
            ring_in(way, s, b).wait_recv()
            if (s + 1, b, way) in ring_list:
                ring(way, s + 1, b).start()

        def advance_both(s, b):
            advance(s, b, 0)
            advance(s, b, 1)

        def s_plane(d):
            to = lax.rem(z + d, NZ)
            return pltpu.make_async_remote_copy(
                stage.at[to], sj.at[y, x, :, pair_lanes(z)], zz_s.at[d - 1], zz_r.at[d - 1],
                device_id=dev(x, y, to, 1), device_id_type=MESH,
            )

        for d in (4, 3, 5, 2, 6, 1, 7):
            staged(lax.rem(z + d, NZ))
            s_plane(d).start()
        staged(z)
        stay = pltpu.make_async_copy(stage.at[z], sj.at[y, x, :, pair_lanes(z)], lo.at[6])
        stay.start()
        advance_both(1, 0)
        other = ai.at[z, 1 - yl]
        pltpu.make_async_remote_copy(other, other, ye_s, ye_r, device_id=partner, device_id_type=MESH).wait_recv()
        ring(0, 1, 1).start()
        ring(1, 1, 1).start()
        for d in (1, 7, 2, 6, 3, 5, 4):
            item = sj.at[y, x, :, pair_lanes(lax.rem(z - d + NZ, NZ))]
            pltpu.make_async_remote_copy(
                item, item, zz_s.at[d - 1], zz_r.at[d - 1], device_id=sibling, device_id_type=MESH
            ).wait_recv()
        stay.wait()
        steps = plane(sj, 1, 32)

        begin, u_first, v_0, u_second, v_1, v_2, v_3, end, ag_sent = steps
        begin()
        advance_both(1, 1)
        u_first()
        v_0()
        advance_both(2, 0)
        u_second()
        advance_both(2, 1)
        v_1()
        v_2()
        advance_both(3, 0)
        v_3()
        advance_both(3, 1)

        def group(offsets, fresh, before_leading, before_columns):
            items = [lax.rem(z + o + NZ, NZ) for o in offsets]

            def put(ref, index, value):
                if fresh:
                    ref[index] = value
                else:
                    ref[index] += value

            def target(it, b):
                return ai[it, b, W : W + 1, :]

            def split_rows(n, c):
                rows = pl.ds(pl.multiple_of(n * N, N), N)
                total = jnp.zeros((N, N), f32)
                for slot, it in enumerate(items):
                    for b in range(2):
                        v = ai[it, b, rows, :]
                        h, l = high_low(v)
                        azh[slot, rows, b * N : (b + 1) * N] = h
                        azl[slot, rows, b * N : (b + 1) * N] = l
                        total = total + v * target(it, b)
                put(acc, (rows, slice(None)), total)
                return c

            def split_leading(n, c):
                rows = pl.ds(pl.multiple_of(W + n * N, N), N)
                total = jnp.zeros((N, N), f32)
                for slot, it in enumerate(items):
                    v = zb[n, :, :, pair_lanes(it)].reshape(N, 2 * N)
                    h, l = high_low(v)
                    azh[slot, rows, :] = h
                    azl[slot, rows, :] = l
                    for b in range(2):
                        total = total + v[:, b * N : (b + 1) * N] * target(it, b)
                put(acc, (rows, slice(None)), total)
                return c

            def left(rows):
                parts = []
                for slot in range(4):
                    h, l = azh[slot, rows, :], azl[slot, rows, :]
                    parts += [h, l, h]
                return jnp.concatenate(parts, 1)

            def panel_columns(n, c):
                rows = pl.ds(pl.multiple_of(W + n * Q, Q), Q)
                parts = []
                for slot in range(4):
                    h, l = azh[slot, rows, :], azl[slot, rows, :]
                    parts += [h, h, l]
                put(gi0, (slice(None), part(n)), bdot(left(pl.ds(0, W)), jnp.concatenate(parts, 1), across))
                return c

            def sums():
                ones = jnp.full((8, N), scale, f32)
                rhs[...] = fdot(ones, acc[:W, :], across)
                top[...] = fdot(ones, acc[W:, :], across)
                give_rhs.start()
                give_top.start()

            def finish_panel():
                gi0[...] = gi0[...] * scale
                gi0[:PANEL, :] += diagonal((PANEL, PANEL), 0, ridge[0:1, :PANEL] * on_i)
                give_gi0.start()

            def columns(n, c):
                parts = []
                for it in items:
                    h, l = high_low(sj[n, :, :, pair_lanes(it)].reshape(Q, 2 * N))
                    parts += [h, h, l]
                put(tg, (slice(None), part(n)), bdot(left(pl.ds(0, W + PANEL)), jnp.concatenate(parts, 1), across))
                if not fresh:

                    @pl.when(n < NS)
                    def _():
                        give_tile(n).start()

                return c

            lax.fori_loop(0, W // N, split_rows, 0)
            before_leading()
            lax.fori_loop(0, PANEL // N, split_leading, 0)
            lax.fori_loop(0, PANEL // Q, panel_columns, 0)
            if not fresh:
                finish_panel()
                sums()
            before_columns()
            lax.fori_loop(0, 4, columns, 0)

        group((0, -1, 1, -2), True, give_z.wait_recv, end)
        advance(4, 0, 0)
        advance(4, 1, 1)
        group((2, -3, 3, 4), False, lambda: None, lambda: None)
        give_inverse.wait_recv()
        give_panel.wait_recv()
        keep_panel.start()
        for n in range(NS, 4):
            update(n)

        steps[-1]()
        for s, b, way in ring_list:
            ring(way, s, b).wait_send()
        trade.wait_send()
        for d in range(1, 16):
            s_piece(d).wait_send()
        for d in range(1, NZ):
            s_plane(d).wait_send()
        give_gi0.wait_send()
        give_rhs.wait_send()
        give_top.wait_send()
        keep_panel.wait()
        for n in range(NS):
            give_tile(n).wait_send()
            give_out(n).wait_recv()
        for n in range(NS, 4):
            keep_out(n).wait()
            give_out(n).wait_send()
        give_red.wait_recv()

    swap.wait_send()
    swap_targets.wait_send()


def on_device(samples, targets, ridge):
    targets, ridge = targets.reshape(1, -1), ridge.reshape(1, -1)
    anywhere = pl.BlockSpec(memory_space=pl.ANY)
    inside = pl.BlockSpec(memory_space=pltpu.VMEM)
    dma = pltpu.SemaphoreType.DMA
    shapes = [(W, W), (W, PANEL), (1, W)]
    trailing, panel, reduced = pl.pallas_call(
        kernel,
        out_shape=[jax.ShapeDtypeStruct(s, f32) for s in shapes],
        in_specs=[inside] * 3,
        out_specs=[anywhere] * len(shapes),
        scratch_shapes=[
            pltpu.VMEM((N, W), f32),
            pltpu.VMEM((2, 8, N), f32),
            pltpu.VMEM((NZ, 2, W + 8, N), f32),
            pltpu.VMEM((4, 4, 64, K), f32),
            pltpu.VMEM((4, 4, 32, K), f32),
            pltpu.VMEM((NZ, 64, 2 * N), f32),
            pltpu.VMEM((8, PANEL), f32),
            pltpu.VMEM((4, W + PANEL, 2 * N), bf16),
            pltpu.VMEM((4, W + PANEL, 2 * N), bf16),
            pltpu.VMEM((W + PANEL, W), f32),
            pltpu.VMEM((W, PANEL), f32),
            pltpu.VMEM((W + PANEL, N), f32),
            pltpu.VMEM((PANEL, PANEL), f32),
            pltpu.VMEM((PANEL, PANEL), f32),
            pltpu.VMEM((N, 2 * N), f32),
            pltpu.VMEM((N, N), f32),
            pltpu.VMEM((W, PANEL), f32),
            pltpu.VMEM((8, W), f32),
            pltpu.VMEM((8, PANEL), f32),
            pltpu.VMEM((1, W), f32),
            dma((2,)), dma((2,)), dma, dma,
            dma((2, 4, 2)), dma((2, 4, 2)),
            dma((16,)), dma((16,)),
            dma((16,)), dma((2,)),
            dma((16,)), dma,
            dma((7,)), dma((7,)),
            dma((2, 20)), dma((2, 20)),
            dma((15,)), dma((15,)), dma((7,)),
        ],
        compiler_params=pltpu.CompilerParams(
            collective_id=0, has_side_effects=True, vmem_limit_bytes=56 << 20
        ),
        name="ridge_panel",
    )(samples, targets, ridge)
    return trailing, panel, reduced.reshape(-1)


def solution(mesh):
    in_specs = (P(("rows", "gc"), "gr"), P(("rows", "gc")), P("gr"))
    out_specs = (P("gr", "gc"), P("gr", None), P("gr"))
    return jax.shard_map(on_device, mesh=mesh, in_specs=in_specs, out_specs=out_specs, check_vma=False)
```

```python
import jax
import jax.numpy as jnp
from jax import lax
from jax.experimental import pallas as pl
from jax.experimental.pallas import tpu as pltpu
from jax.sharding import PartitionSpec as P

f32, bf16 = jnp.float32, jnp.bfloat16
MESH = pl.DeviceIdType.MESH
PANEL = 512
W = 1024
K = 2048
NZ = 8
N = 128
Q = 256
NS = 2


def fdot(a, b, dims=((1,), (0,))):
    return lax.dot_general(a, b, (dims, ((), ())), precision=lax.Precision.HIGHEST, preferred_element_type=f32)


def bdot(a, b, dims=((1,), (0,))):
    return lax.dot_general(a, b, (dims, ((), ())), preferred_element_type=f32)


def high_low(x):
    high = x.astype(bf16)
    return high, (x - high.astype(f32)).astype(bf16)


def split3(x):
    a = x.astype(bf16).astype(f32)
    r = x - a
    b = r.astype(bf16).astype(f32)
    return a, b, r - b


def stack_left(x):
    a, b, c = split3(x)
    return jnp.concatenate([a, a, a, b, b, c], 0).astype(bf16)


def stack_right(x):
    a, b, c = split3(x)
    return jnp.concatenate([a, b, c, a, b, a], 0).astype(bf16)


def dot3(a, b, dims):
    (da,), (db,) = dims
    ah, al = high_low(a)
    bh, bl = high_low(b)
    return bdot(jnp.concatenate([ah, al, ah], da), jnp.concatenate([bh, bh, bl], db), dims)


def row_of(x, i):
    return jnp.broadcast_to(x[i : i + 1, :], (8, x.shape[1]))


def twice(x):
    return jnp.concatenate([x, x], 1)


def strip_factor(s, strip):
    left = strip[:, :N]
    cols = [jnp.take_along_axis(left, jnp.full((8, N), s * 8 + j, jnp.int32), axis=1) for j in range(8)]
    e = {(i, j): row_of(cols[j], i) for j in range(8) for i in range(j, 8)}
    t = [row_of(strip, i) for i in range(8)]
    f, inv, root = {}, [], []
    for k in range(8):
        r = lax.rsqrt(e[k, k])
        r = r * (1.5 - 0.5 * e[k, k] * r * r)
        p = r * r
        p = p * (2.0 - e[k, k] * p)
        inv.append(p)
        root.append(r)
        for i in range(k + 1, 8):
            f[i, k] = e[i, k] * p
        for j in range(k + 1, 8):
            for i in range(j, 8):
                e[i, j] = e[i, j] - f[i, k] * e[j, k]
        for i in range(k + 1, 8):
            t[i] = t[i] - twice(f[i, k]) * t[k]
    y = [None] * 8
    for i in reversed(range(8)):
        acc = t[i] * twice(inv[i])
        for k in range(i + 1, 8):
            acc = acc - twice(f[k, i]) * y[k]
        y[i] = acc
    row = lax.broadcasted_iota(jnp.int32, (8, N), 0)

    def assemble(parts):
        out = parts[0]
        rows = row if out.shape[1] == N else twice(row)
        for i in range(1, 8):
            out = jnp.where(rows == i, parts[i], out)
        return out

    return assemble(y), assemble([t[i][:, N:] * root[i] for i in range(8)]), y


def factor_block(ab, m_ref):
    def body(s, carry):
        strip, left, right = carry
        ab[...] = ab[...] - bdot(left, right)
        whole, inverse_rows, y = strip_factor(s, strip)
        m_ref[pl.ds(pl.multiple_of(s * 8, 8), 8), :] = inverse_rows
        after = lax.rem(s + 1, 16)
        rows = ab[pl.ds(pl.multiple_of(after * 8, 8), 8), :]
        terms = []
        for j in range(8):
            c = jnp.take_along_axis(rows[:, :N], jnp.full((8, N), s * 8 + j, jnp.int32), axis=1)
            terms.append(twice(c) * y[j])
        while len(terms) > 1:
            terms = [terms[i] + terms[i + 1] for i in range(0, len(terms), 2)]
        return rows - terms[0], stack_left(strip[:, :N]).T, stack_right(whole)

    lax.fori_loop(0, 16, body, (ab[0:8, :], jnp.zeros((N, 48), bf16), jnp.zeros((48, 2 * N), bf16)))


def factor_inverse(a, b, ab, m):
    b[...] = jnp.zeros_like(b)
    eye = jnp.where(
        lax.broadcasted_iota(jnp.int32, (N, N), 0) == lax.broadcasted_iota(jnp.int32, (N, N), 1), 1.0, 0.0
    )
    blocks = PANEL // N
    for k in range(blocks):
        now, rest = slice(k * N, (k + 1) * N), slice((k + 1) * N, PANEL)
        ab[:, :N] = a[now, now]
        ab[:, N:] = eye
        factor_block(ab, m)
        b[now, now] = m[...]
        if k:
            b[now, : k * N] = fdot(m[...], b[now, : k * N])
        if k < blocks - 1:
            u = fdot(m[...], a[now, rest])
            a[rest, rest] = a[rest, rest] - fdot(u, u, ((0,), (0,)))
            b[rest, : (k + 1) * N] = b[rest, : (k + 1) * N] - fdot(u, b[now, : (k + 1) * N], ((0,), (0,)))


def kernel(
    samp, targ, ridge,
    out_o, panel_o, red_o,
    chunk, tr, ai, sj, zb, stage, rg, azh, azl, tg, gi0, acc, g00, inverse, ab, mm, panel, red,
    ex_s, ex_r, ye_s, ye_r, si_s, si_r, sc_s, sc_r, zs_s, zs_r, rg_s, rg_r, zz_s, zz_r, ag_s, ag_r, h_s, h_r, lo,
):
    r, i, z = lax.axis_index("rows"), lax.axis_index("gr"), lax.axis_index("gc")
    core, yl = lax.rem(r, 2), r // 2
    x, yh = i // 2, lax.rem(i, 2)
    y = yh * 2 + yl
    p = y * 4 + x
    first, second = core == 0, core == 1
    scale = 1.0 / K
    across, along = ((1,), (1,)), ((1,), (0,))

    def dev(xx, yy, zz, c):
        return {"rows": lax.rem(yy, 2) * 2 + c, "gr": xx * 2 + yy // 2, "gc": zz}

    def up(v, n):
        return lax.rem(v + 1, n)

    def down(v, n):
        return lax.rem(v + n - 1, n)

    sibling = dev(x, y, z, 1 - core)

    barrier = pltpu.get_barrier_semaphore()

    def greet(device):
        pl.semaphore_signal(barrier, inc=1, device_id=device, device_id_type=MESH)

    greet(sibling)
    for d in range(1, NZ):
        greet(dev(x, y, lax.rem(z + d, NZ), core))
    source = jnp.where(i == 0, 1, 0)

    @pl.when(second)
    def _():
        for d in range(1, 16):
            pp = lax.rem(p + d, 16)
            greet(dev(lax.rem(pp, 4), pp // 4, z, 1))
        pl.semaphore_wait(barrier, 23)

    @pl.when(first)
    def _():
        for xx, yy in ((up(x, 4), y), (down(x, 4), y), (x, up(y, 4)), (x, down(y, 4))):
            greet(dev(xx, yy, z, 0))
        for b in range(2):

            @pl.when(jnp.logical_not(jnp.logical_and(i == 0, yl == b)))
            def _():
                greet({"rows": b * 2, "gr": 0, "gc": z})

        pl.semaphore_wait(barrier, 12 + 15 * source)

    mine = pl.ds(pl.multiple_of(core * 64, 64), 64)
    theirs = pl.ds(pl.multiple_of((1 - core) * 64, 64), 64)
    chunk[mine, :] = samp[...]
    tr[core, :, :64] = jnp.broadcast_to(targ[...], (8, 64))
    swap = pltpu.make_async_remote_copy(
        chunk.at[mine], chunk.at[mine], ex_s.at[0], ex_r.at[0], device_id=sibling, device_id_type=MESH
    )
    swap.start()
    swap_targets = pltpu.make_async_remote_copy(
        tr.at[core], tr.at[core], ex_s.at[1], ex_r.at[1], device_id=sibling, device_id_type=MESH
    )
    swap_targets.start()
    pltpu.make_async_remote_copy(
        chunk.at[theirs], chunk.at[theirs], ex_s.at[0], ex_r.at[0], device_id=sibling, device_id_type=MESH
    ).wait_recv()
    own = ai.at[z, yl]
    for b in range(W // N):
        own[b * N : (b + 1) * N, :] = chunk[:, b * N : (b + 1) * N].T
    pltpu.make_async_remote_copy(
        tr.at[1 - core], tr.at[1 - core], ex_s.at[1], ex_r.at[1], device_id=sibling, device_id_type=MESH
    ).wait_recv()
    lane = lax.broadcasted_iota(jnp.int32, (8, N), 1)
    own[W : W + 8, :] = jnp.where(lane < 64, tr[0], pltpu.roll(tr[1], 64, 1))

    def pair_lanes(zz):
        return pl.ds(pl.multiple_of(zz * 2 * N, 2 * N), 2 * N)

    def lanes(zz, b):
        return pl.ds(pl.multiple_of((zz * 2 + b) * N, N), N)

    def plane(buf, c, half_rows, pass_on=None):
        sub = half_rows // 2

        def arrived(copy):
            copy.wait_recv()
            if pass_on is not None:
                pass_on(copy.src_ref)


        def move(h, index, u_off, v_off, off, size, du, dv):
            a, b = (x, y) if h == 0 else (y, x)
            uu, vv = lax.rem(a + u_off + 4, 4), lax.rem(b + v_off + 4, 4)
            tu, tv = lax.rem(a + du + 4, 4), lax.rem(b + dv + 4, 4)
            rows = pl.ds(h * half_rows + off, size)
            item = buf.at[vv, uu, rows] if h == 0 else buf.at[uu, vv, rows]
            to = dev(tu, tv, z, c) if h == 0 else dev(tv, tu, z, c)
            return pltpu.make_async_remote_copy(
                item, item, ag_s.at[h, index], ag_r.at[h, index], device_id=to, device_id_type=MESH
            )

        offsets = (0, -1, 1, 2)

        def u_send(h, n):
            return (
                lambda: move(h, 0, 0, 0, 0, half_rows, 1, 0),
                lambda: move(h, 1, 0, 0, 0, half_rows, -1, 0),
                lambda: move(h, 2, -1, 0, 0, sub, 1, 0),
                lambda: move(h, 3, 1, 0, sub, sub, -1, 0),
            )[n]()

        def u_recv(h, n):
            return (
                lambda: move(h, 0, -1, 0, 0, half_rows, 1, 0),
                lambda: move(h, 1, 1, 0, 0, half_rows, -1, 0),
                lambda: move(h, 2, -2, 0, 0, sub, 1, 0),
                lambda: move(h, 3, 2, 0, sub, sub, -1, 0),
            )[n]()

        def v_send(h, o, n):
            at, u = 4 + 4 * o, offsets[o]
            return (
                lambda: move(h, at, u, 0, 0, half_rows, 0, 1),
                lambda: move(h, at + 1, u, 0, 0, half_rows, 0, -1),
                lambda: move(h, at + 2, u, -1, 0, sub, 0, 1),
                lambda: move(h, at + 3, u, 1, sub, sub, 0, -1),
            )[n]()

        def v_recv(h, o, n):
            at, u = 4 + 4 * o, offsets[o]
            return (
                lambda: move(h, at, u, -1, 0, half_rows, 0, 1),
                lambda: move(h, at + 1, u, 1, 0, half_rows, 0, -1),
                lambda: move(h, at + 2, u, -2, 0, sub, 0, 1),
                lambda: move(h, at + 3, u, 2, sub, sub, 0, -1),
            )[n]()

        def both(step):
            def run():
                for h in range(2):
                    step(h)

            return run

        def begin(h):
            first_copy = u_send(h, 0)
            first_copy.start()
            if pass_on is not None:
                pass_on(first_copy.src_ref)
            u_send(h, 1).start()
            v_send(h, 0, 0).start()
            v_send(h, 0, 1).start()

        def u_first(h):
            for n in range(2):
                arrived(u_recv(h, n))
                u_send(h, n + 2).start()
                v_send(h, n + 1, 0).start()
                v_send(h, n + 1, 1).start()

        def v_forward(o):
            def step(h):
                for n in range(2):
                    arrived(v_recv(h, o, n))
                    v_send(h, o, n + 2).start()

            return step

        def u_second(h):
            arrived(u_recv(h, 2))
            arrived(u_recv(h, 3))
            v_send(h, 3, 0).start()
            v_send(h, 3, 1).start()

        def end(h):
            for o in range(4):
                arrived(v_recv(h, o, 2))
                arrived(v_recv(h, o, 3))

        def sent(h):
            for n in range(4):
                u_send(h, n).wait_send()
                for o in range(4):
                    v_send(h, o, n).wait_send()

        return [both(s) for s in (begin, u_first, v_forward(0), u_second, v_forward(1), v_forward(2), v_forward(3), end, sent)]

    def give(n, src, dst):
        return pltpu.make_async_remote_copy(
            src, dst, h_s.at[n], h_r.at[n], device_id=sibling, device_id_type=MESH
        )

    def part(n):
        return pl.ds(pl.multiple_of(n * Q, Q), Q)

    give_gi0 = give(0, gi0, gi0)
    give_acc = give(1, acc, acc)
    give_z = give(7, zb, zb)
    give_inverse = give(8, inverse, inverse)
    give_panel = give(9, panel, panel)
    give_red = give(10, red, red_o)
    keep_panel = pltpu.make_async_copy(panel, panel_o, lo.at[4])
    keep_red = pltpu.make_async_copy(red, red_o, lo.at[5])

    def give_tile(n):
        return give(3 + n, tg.at[:, part(n)], tg.at[:, part(n)])

    def give_out(n):
        return give(11 + n, tg.at[pl.ds(0, W), part(n)], out_o.at[:, part(n)])

    def keep_out(n):
        return pltpu.make_async_copy(tg.at[pl.ds(0, W), part(n)], out_o.at[:, part(n)], lo.at[n])

    def diagonal(shape, shift, value):
        row = lax.broadcasted_iota(jnp.int32, shape, 0)
        col = lax.broadcasted_iota(jnp.int32, shape, 1)
        return jnp.where(row == col + shift, value, 0.0)

    on_i = jnp.where(i == 0, 1.0, 0.0)
    on_j = jnp.where(z == 0, 1.0, 0.0)
    on_ij = jnp.where(i == z, 1.0, 0.0)

    def update(n):
        right = tg[W:, part(n)] * scale
        if n < 2:
            right = right + diagonal((PANEL, Q), n * Q, rg[0:1, n * Q : (n + 1) * Q] * on_j)
        column_factor = dot3(inverse[...], right, along)
        tile = tg[:W, part(n)] * scale - dot3(panel[...], column_factor, along)
        tg[:W, part(n)] = tile + diagonal((W, Q), n * Q, ridge[0:1, n * Q : (n + 1) * Q] * on_ij)
        keep_out(n).start()
        give_out(n).start()

    @pl.when(first)
    def _():
        def z_piece(d):
            pp = lax.rem(p + d, 16)
            return pltpu.make_async_remote_copy(
                own.at[pl.ds(pl.multiple_of(pp * 32, 32), 32)],
                zb.at[pp // 4, lax.rem(pp, 4), :, lanes(z, yl)],
                zs_s.at[d], zs_r.at[yl],
                device_id=dev(lax.rem(pp, 4), pp // 4, z, 0), device_id_type=MESH,
            )

        def r_piece(d):
            pp = lax.rem(p + d, 16)
            return pltpu.make_async_remote_copy(
                rg, rg, rg_s.at[d], rg_r, device_id=dev(lax.rem(pp, 4), pp // 4, z, 0), device_id_type=MESH
            )

        @pl.when(i == 0)
        def _():
            pltpu.make_async_copy(
                own.at[pl.ds(pl.multiple_of(p * 32, 32), 32)], zb.at[y, x, :, lanes(z, yl)], zs_r.at[yl]
            ).start()
            for d in range(1, 16):
                z_piece(d).start()

            @pl.when(yl == 0)
            def _():
                rg[...] = jnp.broadcast_to(ridge[:, :PANEL], (8, PANEL))
                for d in range(1, 16):
                    r_piece(d).start()

        for b in range(2):
            at = zb.at[y, x, :, lanes(z, b)]
            pltpu.make_async_copy(at, at, zs_r.at[b]).wait()

        def z_plane(d):
            item = zb.at[y, x, :, pair_lanes(z)]
            return pltpu.make_async_remote_copy(
                item, item, zz_s.at[d - 1], zz_r.at[d - 1],
                device_id=dev(x, y, lax.rem(z + d, NZ), 0), device_id_type=MESH,
            )

        for d in (1, 7, 2, 6, 3, 5, 4):
            z_plane(d).start()
        for d in (1, 7, 2, 6, 3, 5, 4):
            item = zb.at[y, x, :, pair_lanes(lax.rem(z - d + NZ, NZ))]
            pltpu.make_async_remote_copy(
                item, item, zz_s.at[d - 1], zz_r.at[d - 1], device_id=sibling, device_id_type=MESH
            ).wait_recv()
        steps = plane(zb, 0, 16, lambda item: give(7, item, item).start())
        for step in steps[:-1]:
            step()

        for b in range(2):
            rows = zb[b * 2 : b * 2 + 2].reshape(256, K)
            g00[b * 256 : (b + 1) * 256, :] = fdot(rows, zb[...].reshape(PANEL, K), across) * scale

        @pl.when(jnp.logical_not(jnp.logical_and(i == 0, yl == 0)))
        def _():
            r_piece(1).wait_recv()

        g00[...] = g00[...] + diagonal((PANEL, PANEL), 0, rg[0:1, :])
        factor_inverse(g00, inverse, ab, mm)
        give_inverse.start()

        give_gi0.wait_recv()
        for b in range(2):
            rows = slice(b * PANEL, (b + 1) * PANEL)
            panel[rows, :] = dot3(gi0[rows, :], inverse[...], across)
        give_panel.start()
        keep_panel.start()
        give_acc.wait_recv()
        ones = jnp.full((8, N), scale, f32)
        rhs = fdot(ones, acc[:W, :], across)
        top = fdot(ones, acc[W:, :], across)
        red[...] = (rhs - fdot(fdot(top, inverse[...], across), panel[...], across))[:1]
        give_red.start()
        keep_red.start()
        for n in range(NS):
            give_tile(n).wait_recv()
            update(n)

        steps[-1]()
        for d in range(1, NZ):
            z_plane(d).wait_send()

        @pl.when(i == 0)
        def _():
            for d in range(1, 16):
                z_piece(d).wait_send()

            @pl.when(yl == 0)
            def _():
                for d in range(1, 16):
                    r_piece(d).wait_send()

        give_z.wait_send()
        give_inverse.wait_send()
        give_panel.wait_send()
        give_red.wait_send()
        keep_panel.wait()
        keep_red.wait()
        for n in range(NS):
            keep_out(n).wait()
            give_out(n).wait_send()
        for n in range(NS, 4):
            give_out(n).wait_recv()

    @pl.when(second)
    def _():
        def ring(way, s, b):
            at = lax.rem(z - s + 1 + NZ, NZ) if way == 0 else lax.rem(z + s - 1, NZ)
            item = ai.at[at, yl if b == 0 else 1 - yl]
            to = dev(x, y, up(z, NZ) if way == 0 else down(z, NZ), 1)
            return pltpu.make_async_remote_copy(
                item, item, si_s.at[way, s - 1, b], si_r.at[way, s - 1, b], device_id=to, device_id_type=MESH
            )

        def ring_in(way, s, b):
            at = lax.rem(z - s + NZ, NZ) if way == 0 else lax.rem(z + s, NZ)
            item = ai.at[at, yl if b == 0 else 1 - yl]
            return pltpu.make_async_remote_copy(
                item, item, si_s.at[way, s - 1, b], si_r.at[way, s - 1, b], device_id=sibling, device_id_type=MESH
            )

        ring_list = [(s, b, way) for s in (1, 2, 3) for b in range(2) for way in range(2)] + [(4, 0, 0), (4, 1, 1)]

        def s_piece(d):
            pp = lax.rem(p + d, 16)
            return pltpu.make_async_remote_copy(
                own.at[pl.ds(pl.multiple_of(pp * 64, 64), 64)],
                stage.at[i, :, pl.ds(pl.multiple_of(yl * N, N), N)],
                sc_s.at[d], sc_r.at[i * 2 + yl],
                device_id=dev(lax.rem(pp, 4), pp // 4, z, 1), device_id_type=MESH,
            )

        for d in range(1, 16):
            s_piece(d).start()
        pltpu.make_async_copy(
            own.at[pl.ds(pl.multiple_of(p * 64, 64), 64)],
            stage.at[i, :, pl.ds(pl.multiple_of(yl * N, N), N)],
            sc_r.at[i * 2 + yl],
        ).start()
        partner = dev(x, yh * 2 + 1 - yl, z, 1)
        trade = pltpu.make_async_remote_copy(own, own, ye_s, ye_r, device_id=partner, device_id_type=MESH)
        trade.start()
        ring(0, 1, 0).start()
        ring(1, 1, 0).start()

        def staged(gr):
            for b in range(2):
                at = stage.at[gr, :, pl.ds(b * N, N)]
                pltpu.make_async_copy(at, at, sc_r.at[gr * 2 + b]).wait()

        def advance(s, b, way):
            ring_in(way, s, b).wait_recv()
            if (s + 1, b, way) in ring_list:
                ring(way, s + 1, b).start()

        def advance_both(s, b):
            advance(s, b, 0)
            advance(s, b, 1)

        def s_plane(d):
            to = lax.rem(z + d, NZ)
            return pltpu.make_async_remote_copy(
                stage.at[to], sj.at[y, x, :, pair_lanes(z)], zz_s.at[d - 1], zz_r.at[d - 1],
                device_id=dev(x, y, to, 1), device_id_type=MESH,
            )

        for d in (4, 3, 5, 2, 6, 1, 7):
            staged(lax.rem(z + d, NZ))
            s_plane(d).start()
        staged(z)
        stay = pltpu.make_async_copy(stage.at[z], sj.at[y, x, :, pair_lanes(z)], lo.at[6])
        stay.start()
        advance_both(1, 0)
        other = ai.at[z, 1 - yl]
        pltpu.make_async_remote_copy(other, other, ye_s, ye_r, device_id=partner, device_id_type=MESH).wait_recv()
        ring(0, 1, 1).start()
        ring(1, 1, 1).start()
        for d in (1, 7, 2, 6, 3, 5, 4):
            item = sj.at[y, x, :, pair_lanes(lax.rem(z - d + NZ, NZ))]
            pltpu.make_async_remote_copy(
                item, item, zz_s.at[d - 1], zz_r.at[d - 1], device_id=sibling, device_id_type=MESH
            ).wait_recv()
        stay.wait()
        steps = plane(sj, 1, 32)

        begin, u_first, v_0, u_second, v_1, v_2, v_3, end, ag_sent = steps
        begin()
        advance_both(1, 1)
        u_first()
        v_0()
        advance_both(2, 0)
        u_second()
        advance_both(2, 1)
        v_1()
        v_2()
        advance_both(3, 0)
        v_3()
        advance_both(3, 1)

        def group(offsets, fresh, before_leading, before_columns):
            items = [lax.rem(z + o + NZ, NZ) for o in offsets]

            def put(ref, index, value):
                if fresh:
                    ref[index] = value
                else:
                    ref[index] += value

            def target(it, b):
                return ai[it, b, W : W + 1, :]

            def split_rows(n, c):
                rows = pl.ds(pl.multiple_of(n * N, N), N)
                total = jnp.zeros((N, N), f32)
                for slot, it in enumerate(items):
                    for b in range(2):
                        v = ai[it, b, rows, :]
                        h, l = high_low(v)
                        azh[slot, rows, b * N : (b + 1) * N] = h
                        azl[slot, rows, b * N : (b + 1) * N] = l
                        total = total + v * target(it, b)
                put(acc, (rows, slice(None)), total)
                return c

            def split_leading(n, c):
                rows = pl.ds(pl.multiple_of(W + n * N, N), N)
                total = jnp.zeros((N, N), f32)
                for slot, it in enumerate(items):
                    v = zb[n, :, :, pair_lanes(it)].reshape(N, 2 * N)
                    h, l = high_low(v)
                    azh[slot, rows, :] = h
                    azl[slot, rows, :] = l
                    for b in range(2):
                        total = total + v[:, b * N : (b + 1) * N] * target(it, b)
                put(acc, (rows, slice(None)), total)
                return c

            def left(rows):
                parts = []
                for slot in range(4):
                    h, l = azh[slot, rows, :], azl[slot, rows, :]
                    parts += [h, l, h]
                return jnp.concatenate(parts, 1)

            def panel_columns(n, c):
                rows = pl.ds(pl.multiple_of(W + n * Q, Q), Q)
                parts = []
                for slot in range(4):
                    h, l = azh[slot, rows, :], azl[slot, rows, :]
                    parts += [h, h, l]
                put(gi0, (slice(None), part(n)), bdot(left(pl.ds(0, W)), jnp.concatenate(parts, 1), across))
                return c

            def finish_panel():
                give_acc.start()
                gi0[...] = gi0[...] * scale
                gi0[:PANEL, :] += diagonal((PANEL, PANEL), 0, ridge[0:1, :PANEL] * on_i)
                give_gi0.start()

            def columns(n, c):
                parts = []
                for it in items:
                    h, l = high_low(sj[n, :, :, pair_lanes(it)].reshape(Q, 2 * N))
                    parts += [h, h, l]
                put(tg, (slice(None), part(n)), bdot(left(pl.ds(0, W + PANEL)), jnp.concatenate(parts, 1), across))
                if not fresh:

                    @pl.when(n < NS)
                    def _():
                        give_tile(n).start()

                return c

            lax.fori_loop(0, W // N, split_rows, 0)
            before_leading()
            lax.fori_loop(0, PANEL // N, split_leading, 0)
            lax.fori_loop(0, PANEL // Q, panel_columns, 0)
            if not fresh:
                finish_panel()
            before_columns()
            lax.fori_loop(0, 4, columns, 0)

        group((0, -1, 1, -2), True, give_z.wait_recv, end)
        advance(4, 0, 0)
        advance(4, 1, 1)
        group((2, -3, 3, 4), False, lambda: None, lambda: None)
        give_inverse.wait_recv()
        give_panel.wait_recv()
        keep_panel.start()
        for n in range(NS, 4):
            update(n)

        steps[-1]()
        for s, b, way in ring_list:
            ring(way, s, b).wait_send()
        trade.wait_send()
        for d in range(1, 16):
            s_piece(d).wait_send()
        for d in range(1, NZ):
            s_plane(d).wait_send()
        give_gi0.wait_send()
        give_acc.wait_send()
        keep_panel.wait()
        for n in range(NS):
            give_tile(n).wait_send()
            give_out(n).wait_recv()
        for n in range(NS, 4):
            keep_out(n).wait()
            give_out(n).wait_send()
        give_red.wait_recv()

    swap.wait_send()
    swap_targets.wait_send()


def hand_out(trailing, panel):
    def copy(t_ref, p_ref, t_out, p_out):
        t_out[...] = t_ref[...]
        p_out[...] = p_ref[...]

    specs = [pl.BlockSpec((Q, W), lambda n: (n, 0)), pl.BlockSpec((Q, PANEL), lambda n: (n, 0))]
    return pl.pallas_call(
        copy,
        grid=(W // Q,),
        out_shape=[jax.ShapeDtypeStruct((W, W), f32), jax.ShapeDtypeStruct((W, PANEL), f32)],
        in_specs=specs,
        out_specs=specs,
        name="hand_out",
    )(trailing, panel)


def on_device(samples, targets, ridge):
    targets, ridge = targets.reshape(1, -1), ridge.reshape(1, -1)
    anywhere = pl.BlockSpec(memory_space=pl.ANY)
    inside = pl.BlockSpec(memory_space=pltpu.VMEM)
    dma = pltpu.SemaphoreType.DMA
    shapes = [(W, W), (W, PANEL), (1, W)]
    trailing, panel, reduced = pl.pallas_call(
        kernel,
        out_shape=[jax.ShapeDtypeStruct(s, f32) for s in shapes],
        in_specs=[inside] * 3,
        out_specs=[anywhere] * len(shapes),
        scratch_shapes=[
            pltpu.VMEM((N, W), f32),
            pltpu.VMEM((2, 8, N), f32),
            pltpu.VMEM((NZ, 2, W + 8, N), f32),
            pltpu.VMEM((4, 4, 64, K), f32),
            pltpu.VMEM((4, 4, 32, K), f32),
            pltpu.VMEM((NZ, 64, 2 * N), f32),
            pltpu.VMEM((8, PANEL), f32),
            pltpu.VMEM((4, W + PANEL, 2 * N), bf16),
            pltpu.VMEM((4, W + PANEL, 2 * N), bf16),
            pltpu.VMEM((W + PANEL, W), f32),
            pltpu.VMEM((W, PANEL), f32),
            pltpu.VMEM((W + PANEL, N), f32),
            pltpu.VMEM((PANEL, PANEL), f32),
            pltpu.VMEM((PANEL, PANEL), f32),
            pltpu.VMEM((N, 2 * N), f32),
            pltpu.VMEM((N, N), f32),
            pltpu.VMEM((W, PANEL), f32),
            pltpu.VMEM((1, W), f32),
            dma((2,)), dma((2,)), dma, dma,
            dma((2, 4, 2)), dma((2, 4, 2)),
            dma((16,)), dma((16,)),
            dma((16,)), dma((2,)),
            dma((16,)), dma,
            dma((7,)), dma((7,)),
            dma((2, 20)), dma((2, 20)),
            dma((15,)), dma((15,)), dma((7,)),
        ],
        compiler_params=pltpu.CompilerParams(
            collective_id=0, has_side_effects=True, vmem_limit_bytes=56 << 20
        ),
        name="ridge_panel",
    )(samples, targets, ridge)
    trailing, panel = hand_out(trailing, panel)
    return trailing, panel, reduced.reshape(-1)


def solution(mesh):
    in_specs = (P(("rows", "gc"), "gr"), P(("rows", "gc")), P("gr"))
    out_specs = (P("gr", "gc"), P("gr", None), P("gr"))
    return jax.shard_map(on_device, mesh=mesh, in_specs=in_specs, out_specs=out_specs, check_vma=False)
```
